32 devices in a mesh: seq: 16 (over z, y, x), tp: 2 (over core).
Axes of the slice: x: 2, y: 2, z: 4, core: 2. Of those that a mesh axis runs over, the one named last changes fastest.
Arguments:
- patches: bfloat16 [1664, 16384], P('tp', 'seq'), may hold values from -400 to 400
- ln_gain: bfloat16 [1664], P('tp'), may hold values from 0.099609375 to 1.8984375
- ln_bias: bfloat16 [1664], P('tp'), may hold values from -3 to 3
- merge_weight: bfloat16 [4, 1664, 1664], P(None, 'tp', 'seq'), may hold values from -0.078125 to 0.078125
- merge_bias: bfloat16 [1664], P('tp'), may hold values from -3 to 3
- targets: int32 [4096], P('seq'), may hold values from 0 to 6143, as said below
- text_embed: bfloat16 [1664, 6144], P('tp', 'seq'), may hold values from -6 to 6
Outputs:
- prompt_embeds: bfloat16 [1664, 6144], P('tp', 'seq')
The draws below stay inside these ranges and needn't reach their ends.
Inputs may be any that keep to these rules, and one draw needn't show every extreme that they name: `targets`: Distinct. The merged rows of one index of seq go to the positions of 8 indices of seq (position p belongs to index p // 384); at most 40 of them to one index, and exactly 40 to some index, from every index.
All inputs are finite; a program needn't handle non-finite values.
Results may differ from the reference program's by a relative error of at most 0.015.
Values may be sent and summed in bfloat16 or wider, within the bound.
A program may use at most 64 MiB of HBM per device.

```python
import math
import jax
import jax.numpy as jnp
from jax import lax

D = 1664
GROUP = 4
TOK_DEV = 1024
MERGED_DEV = 256
PROMPT_DEV = 384
CAP = 40
TOKENS = 16384
MERGED = 4096
PROMPTS = 6144
N_SEQ = 16
N_TP = 2


def draw_patches(key, part):
    key_base, key_cols, key_rows = jax.random.split(key, 3)
    col_scale = jnp.exp(jax.random.uniform(key_cols, (D, 1), jnp.float32) * math.log(10.0))
    row_scale = jnp.exp(jax.random.uniform(key_rows, (1, TOKENS), jnp.float32) * math.log(10.0))
    base_vals = jnp.clip(jax.random.normal(key_base, (D, TOKENS), jnp.float32), -3.0, 3.0)
    values = base_vals * col_scale * row_scale
    return values.astype(jnp.bfloat16)


def draw_targets(key, part):
    devices = N_SEQ
    half_count = devices // 2
    mean_rows = 2 * MERGED_DEV // devices
    spread_rows = mean_rows // 4
    key_offs, key_extra, key_slots, key_order = jax.random.split(key, 4)
    key_pick, key_mix = jax.random.split(key_offs, 2)
    others = jax.random.permutation(key_pick, devices - 1).astype(jnp.int32)
    others = others + (others >= half_count).astype(jnp.int32)
    chosen = jnp.concatenate([jnp.full((1,), half_count, jnp.int32), others[:half_count - 1]])
    offsets = chosen[jax.random.permutation(key_mix, half_count)]
    extra_rows = jax.random.randint(key_extra, (devices, half_count // 2), 0, spread_rows + 1)
    extra_rows = extra_rows.at[:, 0].set(spread_rows)
    row_counts = mean_rows + jnp.concatenate([extra_rows, -extra_rows], axis=1)
    group_ends = jnp.cumsum(row_counts, axis=1)
    group_starts = group_ends - row_counts
    indices = jnp.arange(MERGED_DEV, dtype=jnp.int32)
    group_of = jnp.sum((indices[None, :, None] >= group_ends[:, None, :]).astype(jnp.int32), axis=2)
    start_of = jnp.take_along_axis(group_starts, group_of, axis=1)
    within_group = indices[None, :] - start_of
    source_dev = jnp.arange(devices, dtype=jnp.int32)[:, None]
    target_dev = (source_dev + offsets[group_of]) % devices
    slot_table = jax.vmap(lambda key_item: jax.random.permutation(key_item, PROMPT_DEV))(jax.random.split(key_slots, devices))
    local_pos = slot_table[target_dev, group_of * CAP + within_group]
    global_pos = target_dev * PROMPT_DEV + local_pos
    row_order = jax.vmap(lambda key_item: jax.random.permutation(key_item, MERGED_DEV))(jax.random.split(key_order, devices))
    shuffled = jnp.take_along_axis(global_pos, row_order, axis=1)
    return shuffled.reshape(-1).astype(jnp.int32)


def block_scale(rng, shape, cuts, low, high):
    loudness, own = 1.0, jax.random.fold_in(rng, 6)
    for axis_at, blocks in cuts:
        heights = jnp.exp(jax.random.uniform(jax.random.fold_in(own, axis_at), (blocks,), jnp.float32, low / len(cuts), high / len(cuts)))
        loudness = loudness * jnp.repeat(heights, shape[axis_at] // blocks).reshape([-1 if axis == axis_at else 1 for axis in range(len(shape))])
    return loudness


def bell_draw(rng, shape, width, most, pieces=(), held_as=jnp.bfloat16):
    factor_of = block_scale(rng, shape, pieces, -0.22, 0.18) if pieces else 1.0
    result = jax.random.normal(rng, shape, jnp.float32) * width * factor_of
    return jnp.minimum(jnp.maximum(result, -most), most).astype(held_as)


def setup_inputs(seed: int = 0) -> dict:
    key_list = jax.random.split(jax.random.key(seed), 8)
    return {
        "patches": draw_patches(jax.random.fold_in(key_list[7], 71), 0),
        "ln_gain": jnp.clip(1.0 + 0.18 * jax.random.normal(key_list[1], (D,), jnp.float32), 0.099609375, 1.8984375).astype(jnp.bfloat16),
        "ln_bias": bell_draw(key_list[2], (D,), 0.5, 3.0, ((0, 2),)),
        "merge_weight": bell_draw(key_list[3], (GROUP, D, D), (GROUP * D) ** -0.5, 0.078125, ((1, 2), (2, 16))),
        "merge_bias": bell_draw(key_list[4], (D,), 0.5, 3.0, ((0, 2),)),
        "targets": draw_targets(jax.random.fold_in(key_list[7], 71), 0),
        "text_embed": bell_draw(key_list[6], (D, PROMPTS), 1.0, 6.0, ((0, 2), (1, 16))),
    }


def normalize_block(row_block, gain_row, bias_row):
    values = row_block.astype(jnp.float32)
    row_mean = lax.optimization_barrier(jnp.mean(values, axis=1, keepdims=True))
    centered = values - row_mean
    row_var = lax.optimization_barrier(jnp.mean(centered * centered, axis=1, keepdims=True))
    scaled = centered * lax.rsqrt(row_var + 1e-06) * gain_row + bias_row
    return scaled.astype(jnp.bfloat16)

def reference(patches, ln_gain, ln_bias, merge_weight, merge_bias, targets, text_embed):
    gain_row = ln_gain.astype(jnp.float32)
    bias_row = ln_bias.astype(jnp.float32)
    blocks = patches.T.reshape(N_SEQ, TOK_DEV, D)
    normed = lax.map(lambda row_block: normalize_block(row_block, gain_row, bias_row), blocks)
    grouped = normed.reshape(MERGED, GROUP, D)
    group_width = D // N_TP

    def add_group(step_idx, sum_total):
        first = (jnp.asarray(step_idx) * group_width).astype(jnp.int32)
        inputs = lax.dynamic_slice_in_dim(grouped, first, group_width, 2).reshape(MERGED, GROUP * group_width)
        weights = lax.dynamic_slice_in_dim(merge_weight, first, group_width, 1).reshape(GROUP * group_width, D)
        partial_g = lax.optimization_barrier(jnp.dot(inputs, weights, preferred_element_type=jnp.float32).astype(jnp.bfloat16))
        return sum_total + partial_g.astype(jnp.float32)
    sum_total = lax.fori_loop(0, N_TP, add_group, jnp.zeros((MERGED, D), jnp.float32))
    merged = (sum_total + merge_bias.astype(jnp.float32)).astype(jnp.bfloat16)
    return text_embed.at[:, targets].set(merged.T)
```

```python
import jax
import jax.numpy as jnp
from jax import lax
from jax.sharding import PartitionSpec as P

D = 1664
GROUP = 4


def norm_rows(patches, ln_gain, ln_bias):
    values = patches.astype(jnp.float32)
    width = values.shape[0]
    own_mean = jnp.sum(values, axis=0) / width
    own_dev = values - own_mean[None, :]
    own_square = jnp.sum(own_dev * own_dev, axis=0)
    stats = lax.all_gather(jnp.stack([own_mean, own_square]), "tp", axis=0)
    row_mean = jnp.mean(stats[:, 0], axis=0)
    apart = stats[:, 0] - row_mean[None, :]
    row_var = (jnp.sum(stats[:, 1], axis=0) + width * jnp.sum(apart * apart, axis=0)) / D
    scaled = (values - row_mean[None, :]) * lax.rsqrt(row_var + 1e-06)[None, :] * ln_gain.astype(
        jnp.float32
    )[:, None] + ln_bias.astype(jnp.float32)[:, None]
    return scaled.astype(jnp.bfloat16)


def shards(patches, ln_gain, ln_bias, merge_weight, merge_bias, targets, text_embed):
    seq_count = lax.axis_size("seq")
    planes = [[g + j for j in range(GROUP)] for g in range(0, seq_count, GROUP)]
    columns = [list(range(j, seq_count, GROUP)) for j in range(GROUP)]
    feat_width = patches.shape[0]
    merged_rows = patches.shape[1] // GROUP
    prompt_rows = text_embed.shape[1]
    capacity = 5 * merged_rows // (2 * seq_count)

    weight_part = lax.all_to_all(
        merge_weight, "seq", split_axis=0, concat_axis=2, axis_index_groups=planes, tiled=True
    )[0]
    weight = lax.all_gather(weight_part, "seq", axis=1, axis_index_groups=columns, tiled=True)
    all_targets = lax.all_gather(targets, "seq", axis=0)

    normed = norm_rows(patches, ln_gain, ln_bias)
    by_patch = normed.reshape(feat_width, merged_rows, GROUP).transpose(2, 0, 1)
    tokens = lax.all_to_all(
        by_patch, "seq", split_axis=0, concat_axis=0, axis_index_groups=planes, tiled=True
    )
    target_dev = targets // prompt_rows
    earlier = jnp.arange(merged_rows)[:, None] < jnp.arange(merged_rows)[None, :]
    order_in = jnp.sum((earlier & (target_dev[:, None] == target_dev[None, :])).astype(jnp.int32), axis=0)
    slot_index = target_dev * capacity + order_in
    pick = (jnp.arange(seq_count * capacity)[:, None] == slot_index[None, :]).astype(jnp.bfloat16)
    me = lax.axis_index("seq")
    mine = (all_targets // prompt_rows) == me
    rank = jnp.dot(
        mine.astype(jnp.bfloat16), earlier.astype(jnp.bfloat16), preferred_element_type=jnp.float32
    ).astype(jnp.int32)
    in_slot = mine[:, None, :] & (rank[:, None, :] == jnp.arange(capacity)[None, :, None])
    got_pos = jnp.sum(in_slot * (all_targets % prompt_rows + 1)[:, None, :], axis=2).reshape(-1) - 1
    place = got_pos[:, None] == jnp.arange(prompt_rows)[None, :]
    hit = jnp.any(place, axis=0)

    partial_terms = jnp.einsum(
        "sfm,fc->scm", tokens, weight, preferred_element_type=jnp.float32
    ).astype(jnp.bfloat16)
    halves = lax.psum_scatter(partial_terms, "tp", scatter_dimension=1, tiled=True)
    parts = lax.all_to_all(
        halves, "seq", split_axis=0, concat_axis=0, axis_index_groups=planes, tiled=True
    )
    merged = (
        jnp.sum(parts.astype(jnp.float32), axis=0) + merge_bias.astype(jnp.float32)[:, None]
    ).astype(jnp.bfloat16)
    send = jnp.einsum("sm,cm->sc", pick, merged, preferred_element_type=jnp.float32).astype(jnp.bfloat16)
    got = lax.all_to_all(
        send.reshape(seq_count, capacity, feat_width), "seq", split_axis=0, concat_axis=0, tiled=True
    ).reshape(seq_count * capacity, feat_width)
    image = jnp.einsum(
        "sc,sp->cp", got, place.astype(jnp.bfloat16), preferred_element_type=jnp.float32
    ).astype(jnp.bfloat16)
    return jnp.where(hit[None, :], image, text_embed)


def solution(mesh):
    in_specs = (
        P("tp", "seq"),
        P("tp"),
        P("tp"),
        P(None, "tp", "seq"),
        P("tp"),
        P("seq"),
        P("tp", "seq"),
    )
    out_specs = P("tp", "seq")
    return jax.shard_map(shards, mesh=mesh, in_specs=in_specs, out_specs=out_specs, check_vma=False)
```

```python
import functools

import jax
import jax.numpy as jnp
from jax import lax
from jax.experimental import pallas as pl
from jax.experimental.pallas import tpu as pltpu
from jax.sharding import PartitionSpec as P

D = 1664
GROUP = 4
LANES = 128
MESH = pl.DeviceIdType.MESH
F32 = jnp.float32
BF16 = jnp.bfloat16


def contract(lhs, rhs, lhs_dim, rhs_dim):
    return lax.dot_general(
        lhs, rhs, (((lhs_dim,), (rhs_dim,)), ((), ())), preferred_element_type=F32
    )


def packing(columns, feats):
    main = columns // LANES * LANES
    rest = columns - main
    if main and rest and LANES % rest == 0 and feats % (16 * (LANES // rest)) == 0:
        return main, LANES // rest
    return columns, 0


def merge_kernel(
    nseq, ntp, capacity, slots,
    x_ref, gain_ref, bias_ref, w_ref, mbias_ref, trow_ref, tcol_ref, text_ref,
    out_ref,
    stats, xs, tok, wpl, wmain, wrem, psend, parts, merged, pick, posend, posbuf, send, got, place,
    s_w, r_w, s_z, r_z, s_t, r_t, s_st, r_st, s_p, r_p, s_d, r_d, s_pos, r_pos,
):
    me, tp = lax.axis_index("seq"), lax.axis_index("tp")
    plane, member = me // GROUP, lax.rem(me, GROUP)
    planes = nseq // GROUP
    owned = planes // ntp
    feats, tokens = x_ref.shape
    rows = tokens // GROUP
    prompt_rows = text_ref.shape[1]
    block_cols = wpl.shape[2] * GROUP
    main, fold = packing(block_cols, feats)

    def remote(src, dst, send_sem, recv_sem, seq_id, tp_id):
        return pltpu.make_async_remote_copy(
            src_ref=src, dst_ref=dst, send_sem=send_sem, recv_sem=recv_sem,
            device_id=(seq_id, tp_id), device_id_type=MESH,
        )

    barrier = pltpu.get_barrier_semaphore()

    @pl.loop(0, nseq)
    def _(other):
        @pl.when(other != me)
        def _():
            pl.semaphore_signal(barrier, inc=1, device_id=(other, tp), device_id_type=MESH)

    for other_tp in range(ntp):
        @pl.when(other_tp != tp)
        def _():
            for i in range(GROUP):
                pl.semaphore_signal(
                    barrier, inc=1, device_id=(plane * GROUP + i, other_tp), device_id_type=MESH
                )
    pl.semaphore_wait(barrier, nseq - 1 + GROUP * (ntp - 1))

    def weight_copy(i):
        return remote(
            w_ref.at[i], wpl.at[member], s_w.at[i], r_w.at[member], plane * GROUP + i, tp
        )

    def weight_arrival(i):
        return remote(w_ref.at[i], wpl.at[i], s_w.at[i], r_w.at[i], plane * GROUP + i, tp)

    for i in range(GROUP):
        @pl.when(i != member)
        def _():
            weight_copy(i).start()
    wpl[member] = w_ref[member]

    chunk = 256

    @pl.loop(0, tokens // chunk)
    def _(c):
        at = pl.ds(pl.multiple_of(c * chunk, chunk), chunk)
        values = x_ref[:, at].astype(F32)
        mean = jnp.sum(values, axis=0, keepdims=True) / feats
        apart = values - mean
        stats[tp, 0:1, at] = mean
        stats[tp, 1:2, at] = jnp.sum(apart * apart, axis=0, keepdims=True)

    def stats_copy(other_tp, slot):
        return remote(
            stats.at[slot], stats.at[slot], s_st.at[other_tp], r_st.at[slot], me, other_tp
        )

    for other_tp in range(ntp):
        @pl.when(other_tp != tp)
        def _():
            stats_copy(other_tp, tp).start()

    for i in range(GROUP):
        @pl.when(i != member)
        def _():
            weight_arrival(i).wait_recv()
    block = jnp.concatenate([wpl[i] for i in range(GROUP)], axis=1)
    if fold:
        wmain[plane] = block[:, :main]
        part = feats // fold
        wrem[plane] = jnp.concatenate(
            [block[q * part : (q + 1) * part, main:] for q in range(fold)], axis=1
        )
    else:
        wmain[plane] = block

    def relay(zz, up):
        target = (plane + 1 if up else plane - 1) * GROUP + member
        way = 1 if up else 0
        copies = [remote(wmain.at[zz], wmain.at[zz], s_z.at[way, zz, 0], r_z.at[zz, 0], target, tp)]
        if fold:
            copies.append(
                remote(wrem.at[zz], wrem.at[zz], s_z.at[way, zz, 1], r_z.at[zz, 1], target, tp)
            )
        return copies

    def pass_on(zz, act):
        @pl.when((zz <= plane) & (plane + 1 < planes))
        def _():
            for copy in relay(zz, True):
                act(copy)

        @pl.when((zz >= plane) & (plane > 0))
        def _():
            for copy in relay(zz, False):
                act(copy)

    pass_on(plane, lambda copy: copy.start())

    for other_tp in range(ntp):
        @pl.when(other_tp != tp)
        def _():
            stats_copy(other_tp, other_tp).wait_recv()
    wide = GROUP * LANES
    from_tok = lax.broadcasted_iota(jnp.int32, (wide, wide), 0)
    to_tok = lax.broadcasted_iota(jnp.int32, (wide, wide), 1)
    sorter = (from_tok == GROUP * (to_tok % LANES) + to_tok // LANES).astype(F32).astype(BF16)
    for c in range(tokens // wide):
        at = slice(c * wide, (c + 1) * wide)
        mean = sum(stats[q, 0:1, at] for q in range(ntp)) / ntp
        square = sum(
            stats[q, 1:2, at] + feats * (stats[q, 0:1, at] - mean) ** 2 for q in range(ntp)
        )
        scale = lax.rsqrt(square / (feats * ntp) + 1e-06)
        normed = (
            (x_ref[:, at].astype(F32) - mean) * scale * gain_ref[...] + bias_ref[...]
        ).astype(BF16)
        by_patch = jnp.dot(normed, sorter, preferred_element_type=F32).astype(BF16)
        for i in range(GROUP):
            xs[i, :, c * LANES : (c + 1) * LANES] = by_patch[:, i * LANES : (i + 1) * LANES]

    def token_copy(i, slot, sem):
        return remote(xs.at[i], tok.at[slot], s_t.at[i], r_t.at[sem], plane * GROUP + i, tp)

    for i in range(GROUP):
        @pl.when(i != member)
        def _():
            token_copy(i, member, member).start()
    tok[member] = xs[member]

    dest_row = trow_ref[...] // prompt_rows
    dest_col = tcol_ref[...] // prompt_rows
    first = lax.broadcasted_iota(jnp.int32, (rows, rows), 0)
    second = lax.broadcasted_iota(jnp.int32, (rows, rows), 1)
    same = dest_col == dest_row
    order_row = jnp.sum((same & (first < second)).astype(F32), axis=0, keepdims=True)
    order_col = jnp.sum((same & (second < first)).astype(F32), axis=1, keepdims=True)
    slot_row = dest_row * slots + order_row.astype(jnp.int32)
    slot_col = dest_col * slots + order_col.astype(jnp.int32)
    local_col = (tcol_ref[...] - dest_col * prompt_rows + 1).astype(F32)

    def pos_copy(other, slot):
        return remote(
            posend.at[other], posbuf.at[slot], s_pos.at[other], r_pos.at[slot], other, tp
        )

    @pl.loop(0, nseq)
    def _(other):
        base = other * slots
        slot_at = base + lax.broadcasted_iota(jnp.int32, (slots, rows), 0)
        pick[pl.ds(pl.multiple_of(base, 16), slots), :] = (
            (slot_at == slot_row).astype(F32).astype(BF16)
        )
        lane = lax.broadcasted_iota(jnp.int32, (rows, LANES), 1)
        held = jnp.where((slot_col == base + lane) & (lane < slots), local_col, 0.0)
        posend[other] = jnp.broadcast_to(jnp.sum(held, axis=0, keepdims=True), (8, LANES))

        @pl.when(other != me)
        def _():
            pos_copy(other, me).start()

        @pl.when(other == me)
        def _():
            posbuf[me] = posend[me]

    for i in range(GROUP):
        @pl.when(i != member)
        def _():
            token_copy(i, i, i).wait_recv()

    def part_copy(zz, i):
        home = zz // owned
        return remote(
            psend.at[zz, i],
            parts.at[zz - home * owned, member * ntp + tp],
            s_p.at[zz, i],
            r_p.at[zz - home * owned, member * ntp + tp],
            plane * GROUP + i,
            home,
        )

    def here(zz, i):
        return (zz // owned == tp) & (i == member)

    def use_block(zz):
        if fold:
            lanes = LANES // fold
            rest = jnp.concatenate(
                [wrem[zz][:, q * lanes : (q + 1) * lanes] for q in range(fold)], axis=0
            )
            weight = jnp.concatenate([wmain[zz], rest], axis=1)
        else:
            weight = wmain[zz]
        for i in range(GROUP):
            psend[zz, i] = contract(weight, tok[i], 0, 0).astype(BF16)

            @pl.when(jnp.logical_not(here(zz, i)))
            def _():
                part_copy(zz, i).start()

            @pl.when(here(zz, i))
            def _():
                parts[zz - tp * owned, member * ntp + tp] = psend[zz, i]

    def row_copy(other, slot):
        return remote(
            send.at[other], got.at[slot], s_d.at[other], r_d.at[slot], other, tp
        )

    def part_arrival(b, i, q):
        return remote(
            psend.at[0, 0], parts.at[b, i * ntp + q], s_p.at[0, 0], r_p.at[b, i * ntp + q], me, q
        )

    def place_rows():
        for b in range(owned):
            total = jnp.zeros((block_cols, rows), F32)
            for i in range(GROUP):
                for q in range(ntp):
                    @pl.when((i != member) | (q != tp))
                    def _():
                        part_arrival(b, i, q).wait_recv()
                    total = total + parts[b, i * ntp + q].astype(F32)
            at = slice(b * block_cols, (b + 1) * block_cols)
            merged[at, :] = (total + mbias_ref[at, :]).astype(BF16)

        @pl.loop(0, planes)
        def _(step):
            to = lax.rem(plane + planes // 2 + step, planes)
            size = GROUP * slots
            picked = contract(
                pick[pl.ds(pl.multiple_of(to * size, 16), size), :], merged[...], 1, 1
            ).astype(BF16)
            for i in range(GROUP):
                other = to * GROUP + i
                send[other] = picked[i * slots : (i + 1) * slots]

                @pl.when(other != me)
                def _():
                    row_copy(other, me).start()

                @pl.when(other == me)
                def _():
                    got[me] = send[me]

    def step_of(zz):
        return jnp.where(zz < plane, 2 * (plane - zz) - 1, 2 * (zz - plane))

    last = jnp.maximum(step_of(tp * owned), step_of(tp * owned + owned - 1))
    ready = jnp.minimum(last + 2, 2 * planes - 2)

    @pl.loop(0, 2 * planes - 1)
    def _(step):
        far = (step + 1) // 2
        zz = jnp.where(lax.rem(step, 2) == 1, plane - far, plane + far)

        @pl.when((zz >= 0) & (zz < planes))
        def _():
            @pl.when(zz != plane)
            def _():
                for copy in relay(zz, True):
                    copy.wait_recv()
                pass_on(zz, lambda copy: copy.start())
            use_block(zz)

        @pl.when(step == ready)
        def _():
            place_rows()

    diagonal = lax.broadcasted_iota(jnp.int32, (slots, LANES), 0) == lax.broadcasted_iota(
        jnp.int32, (slots, LANES), 1
    )
    position = lax.broadcasted_iota(jnp.int32, (slots, prompt_rows), 1).astype(F32) + 1.0

    def spots(other, hits):
        @pl.when(other != me)
        def _():
            pos_copy(other, other).wait_recv()
        line = posbuf[other][0:1]
        column = jnp.sum(jnp.where(diagonal, line, 0.0), axis=1, keepdims=True)
        spot = (column == position).astype(F32)
        place[pl.ds(pl.multiple_of(other * slots, 16), slots), :] = spot.astype(BF16)
        return hits + jnp.sum(spot, axis=0, keepdims=True)

    hits = lax.fori_loop(0, nseq, spots, jnp.zeros((1, prompt_rows), F32))

    @pl.loop(0, nseq)
    def _(other):
        @pl.when(other != me)
        def _():
            row_copy(other, other).wait_recv()

    image = contract(got[...].reshape(nseq * slots, feats), place[...], 0, 0)
    out_ref[...] = jnp.where(hits > 0.5, image.astype(BF16), text_ref[...])

    for i in range(GROUP):
        @pl.when(i != member)
        def _():
            weight_copy(i).wait_send()
            token_copy(i, member, member).wait_send()
    for other_tp in range(ntp):
        @pl.when(other_tp != tp)
        def _():
            stats_copy(other_tp, tp).wait_send()

    @pl.loop(0, planes)
    def _(zz):
        pass_on(zz, lambda copy: copy.wait_send())
        for i in range(GROUP):
            @pl.when(jnp.logical_not(here(zz, i)))
            def _():
                part_copy(zz, i).wait_send()

    @pl.loop(0, nseq)
    def _(other):
        @pl.when(other != me)
        def _():
            pos_copy(other, me).wait_send()
            row_copy(other, me).wait_send()


def shards(patches, ln_gain, ln_bias, merge_weight, merge_bias, targets, text_embed):
    nseq, ntp = lax.axis_size("seq"), lax.axis_size("tp")
    feats, tokens = patches.shape
    rows = tokens // GROUP
    shard_cols = merge_weight.shape[2]
    planes = nseq // GROUP
    owned = planes // ntp
    block_cols = GROUP * shard_cols
    prompt_rows = text_embed.shape[1]
    capacity = 5 * rows // (2 * nseq)
    slots = -(-capacity // 16) * 16
    main, fold = packing(block_cols, feats)
    rem_shape = (planes, feats // fold, LANES) if fold else (1, 16, LANES)
    dma = pltpu.SemaphoreType.DMA
    return pl.pallas_call(
        functools.partial(merge_kernel, nseq, ntp, capacity, slots),
        out_shape=jax.ShapeDtypeStruct(text_embed.shape, text_embed.dtype),
        in_specs=[pl.BlockSpec(memory_space=pltpu.VMEM)] * 8,
        out_specs=pl.BlockSpec(memory_space=pltpu.VMEM),
        scratch_shapes=[
            pltpu.VMEM((ntp, 2, tokens), F32),
            pltpu.VMEM((GROUP, feats, rows), BF16),
            pltpu.VMEM((GROUP, feats, rows), BF16),
            pltpu.VMEM((GROUP, feats, shard_cols), BF16),
            pltpu.VMEM((planes, feats, main), BF16),
            pltpu.VMEM(rem_shape, BF16),
            pltpu.VMEM((planes, GROUP, block_cols, rows), BF16),
            pltpu.VMEM((owned, GROUP * ntp, block_cols, rows), BF16),
            pltpu.VMEM((feats, rows), BF16),
            pltpu.VMEM((nseq * slots, rows), BF16),
            pltpu.VMEM((nseq, 8, LANES), F32),
            pltpu.VMEM((nseq, 8, LANES), F32),
            pltpu.VMEM((nseq, slots, feats), BF16),
            pltpu.VMEM((nseq, slots, feats), BF16),
            pltpu.VMEM((nseq * slots, prompt_rows), BF16),
            dma((GROUP,)), dma((GROUP,)),
            dma((2, planes, 2)), dma((planes, 2)),
            dma((GROUP,)), dma((GROUP,)),
            dma((ntp,)), dma((ntp,)),
            dma((planes, GROUP)), dma((owned, GROUP * ntp)),
            dma((nseq,)), dma((nseq,)),
            dma((nseq,)), dma((nseq,)),
        ],
        compiler_params=pltpu.CompilerParams(
            collective_id=0, has_side_effects=True, vmem_limit_bytes=56 * 2**20
        ),
    )(
        patches,
        ln_gain.astype(F32)[:, None],
        ln_bias.astype(F32)[:, None],
        merge_weight,
        merge_bias.astype(F32)[:, None],
        targets[None, :],
        targets[:, None],
        text_embed,
    )


def solution(mesh):
    in_specs = (
        P("tp", "seq"),
        P("tp"),
        P("tp"),
        P(None, "tp", "seq"),
        P("tp"),
        P("seq"),
        P("tp", "seq"),
    )
    out_specs = P("tp", "seq")
    return jax.shard_map(shards, mesh=mesh, in_specs=in_specs, out_specs=out_specs, check_vma=False)
```

```python
import functools

import jax
import jax.numpy as jnp
from jax import lax
from jax.experimental import pallas as pl
from jax.experimental.pallas import tpu as pltpu
from jax.sharding import PartitionSpec as P

D = 1664
GROUP = 4
LANES = 128
MESH = pl.DeviceIdType.MESH
F32 = jnp.float32
BF16 = jnp.bfloat16


def contract(lhs, rhs, lhs_dim, rhs_dim):
    return lax.dot_general(
        lhs, rhs, (((lhs_dim,), (rhs_dim,)), ((), ())), preferred_element_type=F32
    )


def round_up(value, unit):
    return -(-value // unit) * unit


def chunks_of(block_cols):
    first = (block_cols // LANES + 1) // 2 * LANES
    if first and first < block_cols and first % 32 == 0 and block_cols % 32 == 0:
        return [(0, first), (first, block_cols - first)]
    return [(0, block_cols)]


def folding(feats, block_cols):
    main = feats // LANES * LANES
    rest = feats - main
    if main and rest and LANES % rest == 0:
        fold = LANES // rest
        if all(size % (16 * fold) == 0 for _, size in chunks_of(block_cols)):
            return main, fold
    return feats, 0


def payload_rows(slots, size):
    full, rest = divmod(size, LANES)
    total = full * slots
    if rest:
        fold = LANES // rest if LANES % rest == 0 else 1
        total += 8 * (-(-(slots // 8) // fold))
    return round_up(total, 16)


def pack_rows(rows, slots, size):
    full, rest = divmod(size, LANES)
    parts = [rows[:, q * LANES : (q + 1) * LANES] for q in range(full)]
    if rest:
        fold = LANES // rest if LANES % rest == 0 else 1
        groups = [rows[8 * g : 8 * g + 8, full * LANES :] for g in range(slots // 8)]
        for g in range(0, len(groups), fold):
            line = groups[g : g + fold]
            short = LANES - rest * len(line)
            if short:
                line = line + [jnp.zeros((8, short), F32)]
            parts.append(jnp.concatenate(line, axis=1))
    have = sum(part.shape[0] for part in parts)
    if have < payload_rows(slots, size):
        parts.append(jnp.zeros((payload_rows(slots, size) - have, LANES), F32))
    return jnp.concatenate(parts, axis=0)


def unpack_rows(stack, slots, size):
    full, rest = divmod(size, LANES)
    parts = [stack[q * slots : (q + 1) * slots] for q in range(full)]
    if rest:
        fold = LANES // rest if LANES % rest == 0 else 1
        base = full * slots
        groups = []
        for g in range(slots // 8):
            line = base + 8 * (g // fold)
            lane = (g % fold) * rest
            groups.append(stack[line : line + 8, lane : lane + rest])
        parts.append(jnp.concatenate(groups, axis=0))
    return jnp.concatenate(parts, axis=1)


def merge_kernel(
    nseq, ntp, slots, npieces, nchunks,
    x_ref, gain_ref, bias_ref, w_ref, mbias_ref, trow_ref, text_ref,
    out_ref,
    stats, xs, tok, wpl, psend, parts, mcol, pick, posend, posbuf, place,
    s_w, r_w, s_z, r_z, s_t, r_t, s_st, r_st, s_p, r_p, s_d, r_d, s_pos, r_pos,
    *buffers,
):
    me, tp = lax.axis_index("seq"), lax.axis_index("tp")
    plane, member = me // GROUP, lax.rem(me, GROUP)
    planes = nseq // GROUP
    owned = planes // ntp
    feats, tokens = x_ref.shape
    rows = tokens // GROUP
    prompt_rows = text_ref.shape[1]
    shard_cols = wpl.shape[1]
    block_cols = shard_cols * GROUP
    chunks = chunks_of(block_cols)
    main, fold = folding(feats, block_cols)
    per = 2 if fold else 1
    wbuf = [buffers[c * per : (c + 1) * per] for c in range(nchunks)]
    send = buffers[npieces : npieces + nchunks]
    got = buffers[npieces + nchunks :]

    def remote(src, dst, send_sem, recv_sem, seq_id, tp_id):
        return pltpu.make_async_remote_copy(
            src_ref=src, dst_ref=dst, send_sem=send_sem, recv_sem=recv_sem,
            device_id=(seq_id, tp_id), device_id_type=MESH,
        )

    barrier = pltpu.get_barrier_semaphore()

    @pl.loop(0, nseq)
    def _(other):
        @pl.when(other != me)
        def _():
            pl.semaphore_signal(barrier, inc=1, device_id=(other, tp), device_id_type=MESH)

    for other_tp in range(ntp):
        @pl.when(other_tp != tp)
        def _():
            for i in range(GROUP):
                pl.semaphore_signal(
                    barrier, inc=1, device_id=(plane * GROUP + i, other_tp), device_id_type=MESH
                )
    pl.semaphore_wait(barrier, nseq - 1 + GROUP * (ntp - 1))

    def weight_copy(i):
        return remote(
            w_ref.at[i], wpl.at[member], s_w.at[i], r_w.at[member], plane * GROUP + i, tp
        )

    def weight_arrival(i):
        return remote(w_ref.at[i], wpl.at[i], s_w.at[i], r_w.at[i], plane * GROUP + i, tp)

    for i in range(GROUP):
        @pl.when(i != member)
        def _():
            weight_copy(i).start()
    wpl[member] = w_ref[member]

    chunk = 256

    @pl.loop(0, tokens // chunk)
    def _(c):
        at = pl.ds(pl.multiple_of(c * chunk, chunk), chunk)
        values = x_ref[:, at].astype(F32)
        mean = jnp.sum(values, axis=0, keepdims=True) / feats
        apart = values - mean
        stats[tp, 0:1, at] = mean
        stats[tp, 1:2, at] = jnp.sum(apart * apart, axis=0, keepdims=True)

    def stats_copy(other_tp, slot):
        return remote(
            stats.at[slot], stats.at[slot], s_st.at[other_tp], r_st.at[slot], me, other_tp
        )

    for other_tp in range(ntp):
        @pl.when(other_tp != tp)
        def _():
            stats_copy(other_tp, tp).start()

    for i in range(GROUP):
        @pl.when(i != member)
        def _():
            weight_arrival(i).wait_recv()
    block = jnp.concatenate([wpl[i].astype(F32) for i in range(GROUP)], axis=0)
    for c, (row0, size) in enumerate(chunks):
        piece = block[row0 : row0 + size]
        wbuf[c][0][plane] = piece[:, :main].astype(BF16)
        if fold:
            part = size // fold
            wbuf[c][1][plane] = jnp.concatenate(
                [piece[q * part : (q + 1) * part, main:] for q in range(fold)], axis=1
            ).astype(BF16)

    def relay(zz, c, up):
        target = (plane + 1 if up else plane - 1) * GROUP + member
        way = 1 if up else 0
        return [
            remote(
                ref.at[zz], ref.at[zz], s_z.at[way, zz, c * per + q], r_z.at[zz, c * per + q],
                target, tp,
            )
            for q, ref in enumerate(wbuf[c])
        ]

    def pass_on(zz, c, act):
        @pl.when((zz <= plane) & (plane + 1 < planes))
        def _():
            for copy in relay(zz, c, True):
                act(copy)

        @pl.when((zz >= plane) & (plane > 0))
        def _():
            for copy in relay(zz, c, False):
                act(copy)

    def take_and_pass(far, c):
        @pl.loop(0, 2)
        def _(side):
            zz = plane + (2 * side - 1) * far

            @pl.when((zz >= 0) & (zz < planes))
            def _():
                for copy in relay(zz, c, True):
                    copy.wait_recv()
                pass_on(zz, c, lambda copy: copy.start())

    for c in range(nchunks):
        pass_on(plane, c, lambda copy: copy.start())

    for other_tp in range(ntp):
        @pl.when(other_tp != tp)
        def _():
            stats_copy(other_tp, other_tp).wait_recv()
    columns = jnp.concatenate(
        [ref[...].astype(F32) for ref in (gain_ref, bias_ref, mbias_ref)]
        + [jnp.zeros((5, feats), F32)],
        axis=0,
    ).T
    gain, bias = columns[:, 0:1], columns[:, 1:2]
    mcol[...] = jnp.broadcast_to(columns[:, 2:3], (feats, LANES))
    wide = GROUP * LANES
    from_tok = lax.broadcasted_iota(jnp.int32, (wide, wide), 0)
    to_tok = lax.broadcasted_iota(jnp.int32, (wide, wide), 1)
    sorter = (from_tok == GROUP * (to_tok % LANES) + to_tok // LANES).astype(F32).astype(BF16)
    for c in range(tokens // wide):
        at = slice(c * wide, (c + 1) * wide)
        mean = sum(stats[q, 0:1, at] for q in range(ntp)) / ntp
        square = sum(
            stats[q, 1:2, at] + feats * (stats[q, 0:1, at] - mean) ** 2 for q in range(ntp)
        )
        scale = lax.rsqrt(square / (feats * ntp) + 1e-06)
        normed = (
            (x_ref[:, at].astype(F32) - mean) * scale * gain + bias
        ).astype(BF16)
        by_patch = jnp.dot(normed, sorter, preferred_element_type=F32).astype(BF16)
        for i in range(GROUP):
            xs[i, :, c * LANES : (c + 1) * LANES] = by_patch[:, i * LANES : (i + 1) * LANES]

    def token_copy(i, slot, sem):
        return remote(xs.at[i], tok.at[slot], s_t.at[i], r_t.at[sem], plane * GROUP + i, tp)

    for i in range(GROUP):
        @pl.when(i != member)
        def _():
            token_copy(i, member, member).start()
    tok[member] = xs[member]

    trow = trow_ref[...]
    tcol = jnp.broadcast_to(trow.astype(F32), (8, rows)).T[:, 0:1].astype(jnp.int32)
    dest_row = trow // prompt_rows
    dest_col = tcol // prompt_rows
    first = lax.broadcasted_iota(jnp.int32, (rows, rows), 0)
    second = lax.broadcasted_iota(jnp.int32, (rows, rows), 1)
    same = dest_col == dest_row
    order_row = jnp.sum((same & (first < second)).astype(F32), axis=0, keepdims=True)
    order_col = jnp.sum((same & (second < first)).astype(F32), axis=1, keepdims=True)
    slot_row = dest_row * slots + order_row.astype(jnp.int32)
    slot_col = dest_col * slots + order_col.astype(jnp.int32)
    local_col = (tcol - dest_col * prompt_rows + 1).astype(F32)

    @pl.loop(0, planes)
    def _(to):
        size = GROUP * slots
        slot_at = to * size + lax.broadcasted_iota(jnp.int32, (size, rows), 0)
        pick[to] = (slot_at == slot_row).astype(F32).astype(BF16)

    def pos_copy(other, slot):
        return remote(
            posend.at[other], posbuf.at[slot], s_pos.at[other], r_pos.at[slot], other, tp
        )

    @pl.loop(0, nseq)
    def _(other):
        base = other * slots
        lane = lax.broadcasted_iota(jnp.int32, (rows, LANES), 1)
        held = jnp.where((slot_col == base + lane) & (lane < slots), local_col, 0.0)
        posend[other] = jnp.broadcast_to(jnp.sum(held, axis=0, keepdims=True), (8, LANES))

        @pl.when(other != me)
        def _():
            pos_copy(other, me).start()

        @pl.when(other == me)
        def _():
            posbuf[me] = posend[me]

    def part_copy(zz, c, i):
        home = zz // owned
        at = pl.ds(*chunks[c])
        return remote(
            psend.at[zz, i, at],
            parts.at[zz - home * owned, member * ntp + tp, at],
            s_p.at[zz, c, i],
            r_p.at[zz - home * owned, c, member * ntp + tp],
            plane * GROUP + i,
            home,
        )

    def here(zz, i):
        return (zz // owned == tp) & (i == member)

    def use_chunk(zz, c):
        at = pl.ds(*chunks[c])
        weight = wbuf[c][0][zz]
        if fold:
            lanes = LANES // fold
            rest = wbuf[c][1][zz]
            rest = jnp.concatenate(
                [rest[:, q * lanes : (q + 1) * lanes] for q in range(fold)], axis=0
            )
            weight = jnp.concatenate([weight, rest], axis=1)
        for i in range(GROUP):
            psend[zz, i, at] = contract(weight, tok[i], 1, 0).astype(BF16)

            @pl.when(jnp.logical_not(here(zz, i)))
            def _():
                part_copy(zz, c, i).start()

            @pl.when(here(zz, i))
            def _():
                parts[zz - tp * owned, member * ntp + tp, at] = psend[zz, i, at]

    def row_copy(b, c, other, slot):
        return remote(
            send[c].at[b, other], got[c].at[b, slot],
            s_d.at[b, c, other], r_d.at[b, c, slot], other, tp,
        )

    def place_chunk(zz, c):
        b = zz - tp * owned
        row0, size = chunks[c]
        at = pl.ds(row0, size)
        total = jnp.zeros((size, rows), F32)
        for i in range(GROUP):
            for q in range(ntp):
                @pl.when((i != member) | (q != tp))
                def _():
                    remote(
                        psend.at[0, 0, at], parts.at[b, i * ntp + q, at],
                        s_p.at[0, c, 0], r_p.at[b, c, i * ntp + q], me, q,
                    ).wait_recv()
                total = total + parts[b, i * ntp + q, at].astype(F32)
        shift = mcol[pl.ds(pl.multiple_of(b * block_cols + row0, 8), size), :][:, 0:1]
        merged = (total + shift).astype(BF16)

        @pl.loop(0, planes)
        def _(step):
            to = lax.rem(plane + planes // 2 + step, planes)
            picked = contract(pick[to], merged, 1, 1)
            for i in range(GROUP):
                other = to * GROUP + i
                send[c][b, other] = pack_rows(
                    picked[i * slots : (i + 1) * slots], slots, size
                ).astype(BF16)

                @pl.when(other != me)
                def _():
                    row_copy(b, c, other, me).start()

                @pl.when(other == me)
                def _():
                    got[c][b, me] = send[c][b, me]

    def both_sides(far, act):
        @pl.loop(0, 2)
        def _(side):
            zz = plane + (2 * side - 1) * far

            @pl.when((zz >= 0) & (zz < planes) & ((far > 0) | (side == 0)))
            def _():
                act(zz)

    def place_both(far, c):
        def act(zz):
            @pl.when(zz // owned == tp)
            def _():
                place_chunk(zz, c)

        both_sides(far, act)

    for c in range(nchunks):
        take_and_pass(1, c)
    for i in range(GROUP):
        @pl.when(i != member)
        def _():
            token_copy(i, i, i).wait_recv()

    @pl.loop(0, planes)
    def _(far):
        for c in range(nchunks):
            @pl.when(far > 1)
            def _():
                take_and_pass(far, c)
            both_sides(far, lambda zz: use_chunk(zz, c))
            if c:
                place_both(far, c - 1)
            else:
                @pl.when(far > 0)
                def _():
                    place_both(far - 1, nchunks - 1)

    diagonal = lax.broadcasted_iota(jnp.int32, (slots, LANES), 0) == lax.broadcasted_iota(
        jnp.int32, (slots, LANES), 1
    )
    position = (
        lax.broadcasted_iota(jnp.int32, (GROUP * slots, prompt_rows), 1).astype(F32) + 1.0
    )

    def spots(source, hits):
        lines = []
        for i in range(GROUP):
            other = source * GROUP + i

            @pl.when(other != me)
            def _():
                pos_copy(other, other).wait_recv()
            line = posbuf[other][0:1]
            lines.append(jnp.sum(jnp.where(diagonal, line, 0.0), axis=1, keepdims=True))
        spot = (jnp.concatenate(lines, axis=0) == position).astype(F32)
        place[source] = spot.astype(BF16)
        return hits + jnp.sum(spot, axis=0, keepdims=True)

    hits = lax.fori_loop(0, planes, spots, jnp.zeros((1, prompt_rows), F32))
    place_both(planes - 1, nchunks - 1)

    for b in range(owned):
        for c, (row0, size) in enumerate(chunks):
            @pl.loop(0, nseq)
            def _(other):
                @pl.when(other != me)
                def _():
                    row_copy(b, c, other, other).wait_recv()
            arrived = jnp.concatenate(
                [unpack_rows(got[c][b, s].astype(F32), slots, size) for s in range(nseq)], axis=0
            ).astype(BF16)
            image = contract(arrived, place[...].reshape(nseq * slots, prompt_rows), 0, 0)
            at = slice(b * block_cols + row0, b * block_cols + row0 + size)
            out_ref[at, :] = jnp.where(hits > 0.5, image.astype(BF16), text_ref[at, :])

    for i in range(GROUP):
        @pl.when(i != member)
        def _():
            weight_copy(i).wait_send()
            token_copy(i, member, member).wait_send()
    for other_tp in range(ntp):
        @pl.when(other_tp != tp)
        def _():
            stats_copy(other_tp, tp).wait_send()

    @pl.loop(0, planes)
    def _(zz):
        for c in range(nchunks):
            pass_on(zz, c, lambda copy: copy.wait_send())
            for i in range(GROUP):
                @pl.when(jnp.logical_not(here(zz, i)))
                def _():
                    part_copy(zz, c, i).wait_send()

    @pl.loop(0, nseq)
    def _(other):
        @pl.when(other != me)
        def _():
            pos_copy(other, me).wait_send()
            for b in range(owned):
                for c in range(nchunks):
                    row_copy(b, c, other, me).wait_send()


def shards(patches, ln_gain, ln_bias, merge_weight, merge_bias, targets, text_embed):
    nseq, ntp = lax.axis_size("seq"), lax.axis_size("tp")
    feats, tokens = patches.shape
    rows = tokens // GROUP
    shard_cols = merge_weight.shape[2]
    planes = nseq // GROUP
    owned = planes // ntp
    block_cols = GROUP * shard_cols
    prompt_rows = text_embed.shape[1]
    slots = round_up(5 * rows // (2 * nseq), 8)
    chunks = chunks_of(block_cols)
    main, fold = folding(feats, block_cols)
    pieces = []
    for _, size in chunks:
        pieces.append(pltpu.VMEM((planes, size, main), BF16))
        if fold:
            pieces.append(pltpu.VMEM((planes, size // fold, LANES), BF16))
    payloads = [
        pltpu.VMEM((owned, nseq, payload_rows(slots, size), LANES), BF16)
        for _, size in chunks
    ]
    dma = pltpu.SemaphoreType.DMA
    count = len(chunks)
    return pl.pallas_call(
        functools.partial(merge_kernel, nseq, ntp, slots, len(pieces), count),
        out_shape=jax.ShapeDtypeStruct(text_embed.shape, text_embed.dtype),
        in_specs=[pl.BlockSpec(memory_space=pltpu.VMEM)] * 7,
        out_specs=pl.BlockSpec(memory_space=pltpu.VMEM),
        scratch_shapes=[
            pltpu.VMEM((ntp, 2, tokens), F32),
            pltpu.VMEM((GROUP, feats, rows), BF16),
            pltpu.VMEM((GROUP, feats, rows), BF16),
            pltpu.VMEM((GROUP, shard_cols, feats), BF16),
            pltpu.VMEM((planes, GROUP, block_cols, rows), BF16),
            pltpu.VMEM((owned, GROUP * ntp, block_cols, rows), BF16),
            pltpu.VMEM((feats, LANES), F32),
            pltpu.VMEM((planes, GROUP * slots, rows), BF16),
            pltpu.VMEM((nseq, 8, LANES), F32),
            pltpu.VMEM((nseq, 8, LANES), F32),
            pltpu.VMEM((planes, GROUP * slots, prompt_rows), BF16),
            dma((GROUP,)), dma((GROUP,)),
            dma((2, planes, len(pieces))), dma((planes, len(pieces))),
            dma((GROUP,)), dma((GROUP,)),
            dma((ntp,)), dma((ntp,)),
            dma((planes, count, GROUP)), dma((owned, count, GROUP * ntp)),
            dma((owned, count, nseq)), dma((owned, count, nseq)),
            dma((nseq,)), dma((nseq,)),
        ] + pieces + payloads + payloads,
        compiler_params=pltpu.CompilerParams(
            collective_id=0, has_side_effects=True, vmem_limit_bytes=56 * 2**20
        ),
    )(
        patches,
        ln_gain[None, :],
        ln_bias[None, :],
        jnp.swapaxes(merge_weight, 1, 2),
        merge_bias[None, :],
        targets[None, :],
        text_embed,
    )


def solution(mesh):
    in_specs = (
        P("tp", "seq"),
        P("tp"),
        P("tp"),
        P(None, "tp", "seq"),
        P("tp"),
        P("seq"),
        P("tp", "seq"),
    )
    out_specs = P("tp", "seq")
    return jax.shard_map(shards, mesh=mesh, in_specs=in_specs, out_specs=out_specs, check_vma=False)
```

```python
import functools

import jax
import jax.numpy as jnp
from jax import lax
from jax.experimental import pallas as pl
from jax.experimental.pallas import tpu as pltpu
from jax.sharding import PartitionSpec as P

D = 1664
GROUP = 4
LANES = 128
MESH = pl.DeviceIdType.MESH
F32 = jnp.float32
BF16 = jnp.bfloat16


def contract(lhs, rhs, lhs_dim, rhs_dim):
    return lax.dot_general(
        lhs, rhs, (((lhs_dim,), (rhs_dim,)), ((), ())), preferred_element_type=F32
    )


def round_up(value, unit):
    return -(-value // unit) * unit


def chunks_of(block_cols):
    first = (block_cols // LANES + 1) // 2 * LANES
    if first and first < block_cols and first % 32 == 0 and block_cols % 32 == 0:
        return [(0, first), (first, block_cols - first)]
    return [(0, block_cols)]


def folding(feats, block_cols):
    main = feats // LANES * LANES
    rest = feats - main
    if main and rest and LANES % rest == 0:
        fold = LANES // rest
        if all(size % (16 * fold) == 0 for _, size in chunks_of(block_cols)):
            return main, fold
    return feats, 0


def payload_rows(slots, size):
    full, rest = divmod(size, LANES)
    total = full * slots
    if rest:
        fold = LANES // rest if LANES % rest == 0 else 1
        total += 8 * (-(-(slots // 8) // fold))
    return round_up(total, 16)


def pack_rows(rows, slots, size):
    full, rest = divmod(size, LANES)
    parts = [rows[:, q * LANES : (q + 1) * LANES] for q in range(full)]
    if rest:
        fold = LANES // rest if LANES % rest == 0 else 1
        groups = [rows[8 * g : 8 * g + 8, full * LANES :] for g in range(slots // 8)]
        for g in range(0, len(groups), fold):
            line = groups[g : g + fold]
            short = LANES - rest * len(line)
            if short:
                line = line + [jnp.zeros((8, short), F32)]
            parts.append(jnp.concatenate(line, axis=1))
    have = sum(part.shape[0] for part in parts)
    if have < payload_rows(slots, size):
        parts.append(jnp.zeros((payload_rows(slots, size) - have, LANES), F32))
    return jnp.concatenate(parts, axis=0)


def unpack_rows(stack, slots, size):
    full, rest = divmod(size, LANES)
    parts = [stack[q * slots : (q + 1) * slots] for q in range(full)]
    if rest:
        fold = LANES // rest if LANES % rest == 0 else 1
        base = full * slots
        groups = []
        for g in range(slots // 8):
            line = base + 8 * (g // fold)
            lane = (g % fold) * rest
            groups.append(stack[line : line + 8, lane : lane + rest])
        parts.append(jnp.concatenate(groups, axis=0))
    return jnp.concatenate(parts, axis=1)


def merge_kernel(
    nseq, ntp, slots, npieces, nchunks,
    x_ref, vec_ref, w_ref, trow_ref, text_ref,
    out_ref,
    stats, xs, tok, wpl, psend, cores, summed, parts, mcol, pick, posend, posbuf, place,
    s_w, r_w, s_z, r_z, s_t, r_t, s_st, r_st, s_c, r_c, s_p, r_p, s_d, r_d, s_pos, r_pos,
    *buffers,
):
    me, tp = lax.axis_index("seq"), lax.axis_index("tp")
    plane, member = me // GROUP, lax.rem(me, GROUP)
    planes = nseq // GROUP
    owned = planes // ntp
    feats, tokens = x_ref.shape
    rows = tokens // GROUP
    prompt_rows = text_ref.shape[1]
    shard_cols = wpl.shape[1]
    block_cols = shard_cols * GROUP
    chunks = chunks_of(block_cols)
    main, fold = folding(feats, block_cols)
    per = 2 if fold else 1
    wbuf = [buffers[c * per : (c + 1) * per] for c in range(nchunks)]
    send = buffers[npieces : npieces + nchunks]
    got = buffers[npieces + nchunks :]

    def remote(src, dst, send_sem, recv_sem, seq_id, tp_id):
        return pltpu.make_async_remote_copy(
            src_ref=src, dst_ref=dst, send_sem=send_sem, recv_sem=recv_sem,
            device_id=(seq_id, tp_id), device_id_type=MESH,
        )

    barrier = pltpu.get_barrier_semaphore()

    @pl.loop(0, nseq)
    def _(other):
        @pl.when(other != me)
        def _():
            pl.semaphore_signal(barrier, inc=1, device_id=(other, tp), device_id_type=MESH)

    for other_tp in range(ntp):
        @pl.when(other_tp != tp)
        def _():
            for i in range(GROUP):
                pl.semaphore_signal(
                    barrier, inc=1, device_id=(plane * GROUP + i, other_tp), device_id_type=MESH
                )
    pl.semaphore_wait(barrier, nseq - 1 + GROUP * (ntp - 1))

    def weight_copy(i):
        return remote(
            w_ref.at[i], wpl.at[member], s_w.at[i], r_w.at[member], plane * GROUP + i, tp
        )

    def weight_arrival(i):
        return remote(w_ref.at[i], wpl.at[i], s_w.at[i], r_w.at[i], plane * GROUP + i, tp)

    for i in range(GROUP):
        @pl.when(i != member)
        def _():
            weight_copy(i).start()
    wpl[member] = w_ref[member]

    chunk = 256

    @pl.loop(0, tokens // chunk)
    def _(c):
        at = pl.ds(pl.multiple_of(c * chunk, chunk), chunk)
        values = x_ref[:, at].astype(F32)
        mean = jnp.sum(values, axis=0, keepdims=True) / feats
        apart = values - mean
        stats[tp, 0:1, at] = mean
        stats[tp, 1:2, at] = jnp.sum(apart * apart, axis=0, keepdims=True)

    def stats_copy(other_tp, slot):
        return remote(
            stats.at[slot], stats.at[slot], s_st.at[other_tp], r_st.at[slot], me, other_tp
        )

    for other_tp in range(ntp):
        @pl.when(other_tp != tp)
        def _():
            stats_copy(other_tp, tp).start()

    for i in range(GROUP):
        @pl.when(i != member)
        def _():
            weight_arrival(i).wait_recv()
    block = jnp.concatenate([wpl[i].astype(F32) for i in range(GROUP)], axis=0)
    for c, (row0, size) in enumerate(chunks):
        piece = block[row0 : row0 + size]
        wbuf[c][0][plane] = piece[:, :main].astype(BF16)
        if fold:
            part = size // fold
            wbuf[c][1][plane] = jnp.concatenate(
                [piece[q * part : (q + 1) * part, main:] for q in range(fold)], axis=1
            ).astype(BF16)

    def relay(zz, c, up):
        target = (plane + 1 if up else plane - 1) * GROUP + member
        way = 1 if up else 0
        return [
            remote(
                ref.at[zz], ref.at[zz], s_z.at[way, zz, c * per + q], r_z.at[zz, c * per + q],
                target, tp,
            )
            for q, ref in enumerate(wbuf[c])
        ]

    def pass_on(zz, c, act):
        @pl.when((zz <= plane) & (plane + 1 < planes))
        def _():
            for copy in relay(zz, c, True):
                act(copy)

        @pl.when((zz >= plane) & (plane > 0))
        def _():
            for copy in relay(zz, c, False):
                act(copy)

    def take_and_pass(far, c):
        @pl.loop(0, 2)
        def _(side):
            zz = plane + (2 * side - 1) * far

            @pl.when((zz >= 0) & (zz < planes))
            def _():
                for copy in relay(zz, c, True):
                    copy.wait_recv()
                pass_on(zz, c, lambda copy: copy.start())

    for c in range(nchunks):
        pass_on(plane, c, lambda copy: copy.start())

    for other_tp in range(ntp):
        @pl.when(other_tp != tp)
        def _():
            stats_copy(other_tp, other_tp).wait_recv()
    columns = jnp.concatenate(
        [vec_ref[:, q * feats : (q + 1) * feats] for q in range(3)] + [jnp.zeros((5, feats), F32)],
        axis=0,
    ).T
    gain, bias = columns[:, 0:1], columns[:, 1:2]
    mcol[...] = jnp.broadcast_to(columns[:, 2:3], (feats, LANES))
    wide = GROUP * LANES
    from_tok = lax.broadcasted_iota(jnp.int32, (wide, wide), 0)
    to_tok = lax.broadcasted_iota(jnp.int32, (wide, wide), 1)
    sorter = (from_tok == GROUP * (to_tok % LANES) + to_tok // LANES).astype(F32).astype(BF16)
    for c in range(tokens // wide):
        at = slice(c * wide, (c + 1) * wide)
        mean = sum(stats[q, 0:1, at] for q in range(ntp)) / ntp
        square = sum(
            stats[q, 1:2, at] + feats * (stats[q, 0:1, at] - mean) ** 2 for q in range(ntp)
        )
        scale = lax.rsqrt(square / (feats * ntp) + 1e-06)
        normed = (
            (x_ref[:, at].astype(F32) - mean) * scale * gain + bias
        ).astype(BF16)
        by_patch = jnp.dot(normed, sorter, preferred_element_type=F32).astype(BF16)
        for i in range(GROUP):
            xs[i, :, c * LANES : (c + 1) * LANES] = by_patch[:, i * LANES : (i + 1) * LANES]

    def token_copy(i, slot, sem):
        return remote(xs.at[i], tok.at[slot], s_t.at[i], r_t.at[sem], plane * GROUP + i, tp)

    for i in range(GROUP):
        @pl.when(i != member)
        def _():
            token_copy(i, member, member).start()
    tok[member] = xs[member]

    trow = trow_ref[...]
    tcol = jnp.broadcast_to(trow.astype(F32), (8, rows)).T[:, 0:1].astype(jnp.int32)
    dest_row = trow // prompt_rows
    dest_col = tcol // prompt_rows
    first = lax.broadcasted_iota(jnp.int32, (rows, rows), 0)
    second = lax.broadcasted_iota(jnp.int32, (rows, rows), 1)
    same = dest_col == dest_row
    order_row = jnp.sum((same & (first < second)).astype(F32), axis=0, keepdims=True)
    order_col = jnp.sum((same & (second < first)).astype(F32), axis=1, keepdims=True)
    slot_row = dest_row * slots + order_row.astype(jnp.int32)
    slot_col = dest_col * slots + order_col.astype(jnp.int32)
    local_col = (tcol - dest_col * prompt_rows + 1).astype(F32)

    @pl.loop(0, planes)
    def _(to):
        size = GROUP * slots
        slot_at = to * size + lax.broadcasted_iota(jnp.int32, (size, rows), 0)
        pick[to] = (slot_at == slot_row).astype(F32).astype(BF16)

    def pos_copy(other, slot):
        return remote(
            posend.at[other], posbuf.at[slot], s_pos.at[other], r_pos.at[slot], other, tp
        )

    @pl.loop(0, nseq)
    def _(other):
        base = other * slots
        lane = lax.broadcasted_iota(jnp.int32, (rows, LANES), 1)
        held = jnp.where((slot_col == base + lane) & (lane < slots), local_col, 0.0)
        posend[other] = jnp.broadcast_to(jnp.sum(held, axis=0, keepdims=True), (8, LANES))

        @pl.when(other != me)
        def _():
            pos_copy(other, me).start()

        @pl.when(other == me)
        def _():
            posbuf[me] = posend[me]

    def core_copy(zz, c):
        home = zz // owned
        at = pl.ds(*chunks[c])
        return remote(
            psend.at[zz, :, at], cores.at[zz - home * owned, tp, :, at],
            s_c.at[zz, c], r_c.at[zz - home * owned, c, tp], me, home,
        )

    def part_copy(b, c, i):
        at = pl.ds(*chunks[c])
        return remote(
            summed.at[b, i, at], parts.at[b, member, at],
            s_p.at[b, c, i], r_p.at[b, c, member], plane * GROUP + i, tp,
        )

    def use_chunk(zz, c):
        at = pl.ds(*chunks[c])
        weight = wbuf[c][0][zz]
        if fold:
            lanes = LANES // fold
            rest = wbuf[c][1][zz]
            rest = jnp.concatenate(
                [rest[:, q * lanes : (q + 1) * lanes] for q in range(fold)], axis=0
            )
            weight = jnp.concatenate([weight, rest], axis=1)
        for i in range(GROUP):
            psend[zz, i, at] = contract(weight, tok[i], 1, 0).astype(BF16)

        @pl.when(zz // owned != tp)
        def _():
            core_copy(zz, c).start()

    def join_chunk(zz, c):
        b = zz - tp * owned
        at = pl.ds(*chunks[c])
        for q in range(ntp):
            @pl.when(q != tp)
            def _():
                remote(
                    psend.at[zz, :, at], cores.at[b, q, :, at], s_c.at[zz, c], r_c.at[b, c, q], me, q
                ).wait_recv()

            @pl.when(q == tp)
            def _():
                cores[b, q, :, at] = psend[zz, :, at]
        for i in range(GROUP):
            total = sum(cores[b, q, i, at].astype(F32) for q in range(ntp))
            summed[b, i, at] = total.astype(BF16)

            @pl.when(i != member)
            def _():
                part_copy(b, c, i).start()

            @pl.when(i == member)
            def _():
                parts[b, member, at] = summed[b, i, at]

    def row_copy(b, c, other, slot):
        return remote(
            send[c].at[b, other], got[c].at[b, slot],
            s_d.at[b, c, other], r_d.at[b, c, slot], other, tp,
        )

    def place_chunk(zz, c):
        b = zz - tp * owned
        row0, size = chunks[c]
        at = pl.ds(row0, size)
        total = jnp.zeros((size, rows), F32)
        for i in range(GROUP):
            @pl.when(i != member)
            def _():
                remote(
                    summed.at[b, i, at], parts.at[b, i, at],
                    s_p.at[b, c, i], r_p.at[b, c, i], plane * GROUP + i, tp,
                ).wait_recv()
            total = total + parts[b, i, at].astype(F32)
        shift = mcol[pl.ds(pl.multiple_of(b * block_cols + row0, 8), size), :][:, 0:1]
        merged = (total + shift).astype(BF16)

        @pl.loop(0, planes)
        def _(step):
            to = lax.rem(plane + planes // 2 + step, planes)
            picked = contract(pick[to], merged, 1, 1)
            for i in range(GROUP):
                other = to * GROUP + i
                send[c][b, other] = pack_rows(
                    picked[i * slots : (i + 1) * slots], slots, size
                ).astype(BF16)

                @pl.when(other != me)
                def _():
                    row_copy(b, c, other, me).start()

                @pl.when(other == me)
                def _():
                    got[c][b, me] = send[c][b, me]

    def both_sides(far, act):
        @pl.loop(0, 2)
        def _(side):
            zz = plane + (2 * side - 1) * far

            @pl.when((zz >= 0) & (zz < planes) & ((far > 0) | (side == 0)))
            def _():
                act(zz)

    def owned_sides(far, c, act):
        def act_owned(zz):
            @pl.when(zz // owned == tp)
            def _():
                act(zz, c)

        both_sides(far, act_owned)

    for c in range(nchunks):
        take_and_pass(1, c)
    for i in range(GROUP):
        @pl.when(i != member)
        def _():
            token_copy(i, i, i).wait_recv()

    @pl.loop(0, planes)
    def _(far):
        for c in range(nchunks):
            @pl.when(far > 1)
            def _():
                take_and_pass(far, c)
            both_sides(far, lambda zz: use_chunk(zz, c))
            if c:
                owned_sides(far, c - 1, place_chunk)
            else:
                @pl.when(far > 0)
                def _():
                    owned_sides(far - 1, nchunks - 1, place_chunk)
            owned_sides(far, c, join_chunk)

    diagonal = lax.broadcasted_iota(jnp.int32, (slots, LANES), 0) == lax.broadcasted_iota(
        jnp.int32, (slots, LANES), 1
    )
    position = (
        lax.broadcasted_iota(jnp.int32, (GROUP * slots, prompt_rows), 1).astype(F32) + 1.0
    )

    def spots(source, hits):
        lines = []
        for i in range(GROUP):
            other = source * GROUP + i

            @pl.when(other != me)
            def _():
                pos_copy(other, other).wait_recv()
            line = posbuf[other][0:1]
            lines.append(jnp.sum(jnp.where(diagonal, line, 0.0), axis=1, keepdims=True))
        spot = (jnp.concatenate(lines, axis=0) == position).astype(F32)
        place[source] = spot.astype(BF16)
        return hits + jnp.sum(spot, axis=0, keepdims=True)

    hits = lax.fori_loop(0, planes, spots, jnp.zeros((1, prompt_rows), F32))
    owned_sides(planes - 1, nchunks - 1, place_chunk)

    for b in range(owned):
        for c, (row0, size) in enumerate(chunks):
            @pl.loop(0, nseq)
            def _(other):
                @pl.when(other != me)
                def _():
                    row_copy(b, c, other, other).wait_recv()
            arrived = jnp.concatenate(
                [unpack_rows(got[c][b, s].astype(F32), slots, size) for s in range(nseq)], axis=0
            ).astype(BF16)
            image = contract(arrived, place[...].reshape(nseq * slots, prompt_rows), 0, 0)
            at = slice(b * block_cols + row0, b * block_cols + row0 + size)
            out_ref[at, :] = jnp.where(hits > 0.5, image.astype(BF16), text_ref[at, :])

    for i in range(GROUP):
        @pl.when(i != member)
        def _():
            weight_copy(i).wait_send()
            token_copy(i, member, member).wait_send()
    for other_tp in range(ntp):
        @pl.when(other_tp != tp)
        def _():
            stats_copy(other_tp, tp).wait_send()

    @pl.loop(0, planes)
    def _(zz):
        for c in range(nchunks):
            pass_on(zz, c, lambda copy: copy.wait_send())

            @pl.when(zz // owned != tp)
            def _():
                core_copy(zz, c).wait_send()

            @pl.when(zz // owned == tp)
            def _():
                for i in range(GROUP):
                    @pl.when(i != member)
                    def _():
                        part_copy(zz - tp * owned, c, i).wait_send()

    @pl.loop(0, nseq)
    def _(other):
        @pl.when(other != me)
        def _():
            pos_copy(other, me).wait_send()
            for b in range(owned):
                for c in range(nchunks):
                    row_copy(b, c, other, me).wait_send()


def shards(patches, ln_gain, ln_bias, merge_weight, merge_bias, targets, text_embed):
    nseq, ntp = lax.axis_size("seq"), lax.axis_size("tp")
    feats, tokens = patches.shape
    rows = tokens // GROUP
    shard_cols = merge_weight.shape[2]
    planes = nseq // GROUP
    owned = planes // ntp
    block_cols = GROUP * shard_cols
    prompt_rows = text_embed.shape[1]
    slots = round_up(5 * rows // (2 * nseq), 8)
    chunks = chunks_of(block_cols)
    main, fold = folding(feats, block_cols)
    pieces = []
    for _, size in chunks:
        pieces.append(pltpu.VMEM((planes, size, main), BF16))
        if fold:
            pieces.append(pltpu.VMEM((planes, size // fold, LANES), BF16))
    payloads = [
        pltpu.VMEM((owned, nseq, payload_rows(slots, size), LANES), BF16)
        for _, size in chunks
    ]
    dma = pltpu.SemaphoreType.DMA
    count = len(chunks)
    return pl.pallas_call(
        functools.partial(merge_kernel, nseq, ntp, slots, len(pieces), count),
        out_shape=jax.ShapeDtypeStruct(text_embed.shape, text_embed.dtype),
        in_specs=[pl.BlockSpec(memory_space=pltpu.VMEM)] * 5,
        out_specs=pl.BlockSpec(memory_space=pltpu.VMEM),
        scratch_shapes=[
            pltpu.VMEM((ntp, 2, tokens), F32),
            pltpu.VMEM((GROUP, feats, rows), BF16),
            pltpu.VMEM((GROUP, feats, rows), BF16),
            pltpu.VMEM((GROUP, shard_cols, feats), BF16),
            pltpu.VMEM((planes, GROUP, block_cols, rows), BF16),
            pltpu.VMEM((owned, ntp, GROUP, block_cols, rows), BF16),
            pltpu.VMEM((owned, GROUP, block_cols, rows), BF16),
            pltpu.VMEM((owned, GROUP, block_cols, rows), BF16),
            pltpu.VMEM((feats, LANES), F32),
            pltpu.VMEM((planes, GROUP * slots, rows), BF16),
            pltpu.VMEM((nseq, 8, LANES), F32),
            pltpu.VMEM((nseq, 8, LANES), F32),
            pltpu.VMEM((planes, GROUP * slots, prompt_rows), BF16),
            dma((GROUP,)), dma((GROUP,)),
            dma((2, planes, len(pieces))), dma((planes, len(pieces))),
            dma((GROUP,)), dma((GROUP,)),
            dma((ntp,)), dma((ntp,)),
            dma((planes, count)), dma((owned, count, ntp)),
            dma((owned, count, GROUP)), dma((owned, count, GROUP)),
            dma((owned, count, nseq)), dma((owned, count, nseq)),
            dma((nseq,)), dma((nseq,)),
        ] + pieces + payloads + payloads,
        compiler_params=pltpu.CompilerParams(
            collective_id=0, has_side_effects=True, vmem_limit_bytes=56 * 2**20
        ),
    )(
        patches,
        jnp.concatenate([v.astype(F32) for v in (ln_gain, ln_bias, merge_bias)])[None, :],
        jnp.swapaxes(merge_weight, 1, 2),
        targets[None, :],
        text_embed,
    )


def solution(mesh):
    in_specs = (
        P("tp", "seq"),
        P("tp"),
        P("tp"),
        P(None, "tp", "seq"),
        P("tp"),
        P("seq"),
        P("tp", "seq"),
    )
    out_specs = P("tp", "seq")
    return jax.shard_map(shards, mesh=mesh, in_specs=in_specs, out_specs=out_specs, check_vma=False)
```

```python
import functools

import jax
import jax.numpy as jnp
from jax import lax
from jax.experimental import pallas as pl
from jax.experimental.pallas import tpu as pltpu
from jax.sharding import PartitionSpec as P

D = 1664
GROUP = 4
LANES = 128
MESH = pl.DeviceIdType.MESH
F32 = jnp.float32
BF16 = jnp.bfloat16


def contract(lhs, rhs, lhs_dim, rhs_dim):
    return lax.dot_general(
        lhs, rhs, (((lhs_dim,), (rhs_dim,)), ((), ())), preferred_element_type=F32
    )


def round_up(value, unit):
    return -(-value // unit) * unit


def chunks_of(block_cols):
    first = (block_cols // LANES + 1) // 2 * LANES
    if first and first < block_cols and first % 32 == 0 and block_cols % 32 == 0:
        return [(0, first), (first, block_cols - first)]
    return [(0, block_cols)]


def folding(feats, block_cols):
    main = feats // LANES * LANES
    rest = feats - main
    if main and rest and LANES % rest == 0:
        fold = LANES // rest
        if all(size % (16 * fold) == 0 for _, size in chunks_of(block_cols)):
            return main, fold
    return feats, 0


def payload_rows(slots, size):
    full, rest = divmod(size, LANES)
    total = full * slots
    if rest:
        fold = LANES // rest if LANES % rest == 0 else 1
        total += 8 * (-(-(slots // 8) // fold))
    return round_up(total, 16)


def pack_rows(rows, slots, size):
    full, rest = divmod(size, LANES)
    parts = [rows[:, q * LANES : (q + 1) * LANES] for q in range(full)]
    if rest:
        fold = LANES // rest if LANES % rest == 0 else 1
        groups = [rows[8 * g : 8 * g + 8, full * LANES :] for g in range(slots // 8)]
        for g in range(0, len(groups), fold):
            line = groups[g : g + fold]
            short = LANES - rest * len(line)
            if short:
                line = line + [jnp.zeros((8, short), F32)]
            parts.append(jnp.concatenate(line, axis=1))
    have = sum(part.shape[0] for part in parts)
    if have < payload_rows(slots, size):
        parts.append(jnp.zeros((payload_rows(slots, size) - have, LANES), F32))
    return jnp.concatenate(parts, axis=0)


def unpack_rows(stack, slots, size):
    full, rest = divmod(size, LANES)
    parts = [stack[q * slots : (q + 1) * slots] for q in range(full)]
    if rest:
        fold = LANES // rest if LANES % rest == 0 else 1
        base = full * slots
        groups = []
        for g in range(slots // 8):
            line = base + 8 * (g // fold)
            lane = (g % fold) * rest
            groups.append(stack[line : line + 8, lane : lane + rest])
        parts.append(jnp.concatenate(groups, axis=0))
    return jnp.concatenate(parts, axis=1)


def merge_kernel(
    nseq, ntp, slots, npieces, nchunks,
    x_ref, vec_ref, w_ref, trow_ref, text_ref,
    out_ref,
    stats, xs, tok, wpl, psend, cores, summed, parts, mcol, pick, posend, posbuf, place,
    s_w, r_w, s_z, r_z, s_t, r_t, s_st, r_st, s_c, r_c, s_p, r_p, s_d, r_d, s_pos, r_pos,
    *buffers,
):
    me, tp = lax.axis_index("seq"), lax.axis_index("tp")
    plane, member = me // GROUP, lax.rem(me, GROUP)
    planes = nseq // GROUP
    owned = planes // ntp
    feats, tokens = x_ref.shape
    rows = tokens // GROUP
    prompt_rows = text_ref.shape[1]
    shard_cols = wpl.shape[1]
    block_cols = shard_cols * GROUP
    chunks = chunks_of(block_cols)
    main, fold = folding(feats, block_cols)
    per = 2 if fold else 1
    wbuf = [buffers[c * per : (c + 1) * per] for c in range(nchunks)]
    send = buffers[npieces : npieces + nchunks]
    got = buffers[npieces + nchunks :]

    def remote(src, dst, send_sem, recv_sem, seq_id, tp_id):
        return pltpu.make_async_remote_copy(
            src_ref=src, dst_ref=dst, send_sem=send_sem, recv_sem=recv_sem,
            device_id=(seq_id, tp_id), device_id_type=MESH,
        )

    barrier = pltpu.get_barrier_semaphore()

    @pl.loop(0, nseq)
    def _(other):
        @pl.when(other != me)
        def _():
            pl.semaphore_signal(barrier, inc=1, device_id=(other, tp), device_id_type=MESH)

    for other_tp in range(ntp):
        @pl.when(other_tp != tp)
        def _():
            for i in range(GROUP):
                pl.semaphore_signal(
                    barrier, inc=1, device_id=(plane * GROUP + i, other_tp), device_id_type=MESH
                )
    pl.semaphore_wait(barrier, nseq - 1 + GROUP * (ntp - 1))

    def weight_copy(i):
        return remote(
            w_ref.at[i], wpl.at[member], s_w.at[i], r_w.at[member], plane * GROUP + i, tp
        )

    def weight_arrival(i):
        return remote(w_ref.at[i], wpl.at[i], s_w.at[i], r_w.at[i], plane * GROUP + i, tp)

    for i in range(GROUP):
        @pl.when(i != member)
        def _():
            weight_copy(i).start()
    wpl[member] = w_ref[member]

    chunk = 256

    @pl.loop(0, tokens // chunk)
    def _(c):
        at = pl.ds(pl.multiple_of(c * chunk, chunk), chunk)
        values = x_ref[:, at].astype(F32)
        mean = jnp.sum(values, axis=0, keepdims=True) / feats
        apart = values - mean
        stats[tp, 0:1, at] = mean
        stats[tp, 1:2, at] = jnp.sum(apart * apart, axis=0, keepdims=True)

    def stats_copy(other_tp, slot):
        return remote(
            stats.at[slot], stats.at[slot], s_st.at[other_tp], r_st.at[slot], me, other_tp
        )

    for other_tp in range(ntp):
        @pl.when(other_tp != tp)
        def _():
            stats_copy(other_tp, tp).start()

    for i in range(GROUP):
        @pl.when(i != member)
        def _():
            weight_arrival(i).wait_recv()
    block = jnp.concatenate([wpl[i].astype(F32) for i in range(GROUP)], axis=0)
    for c, (row0, size) in enumerate(chunks):
        piece = block[row0 : row0 + size]
        wbuf[c][0][plane] = piece[:, :main].astype(BF16)
        if fold:
            part = size // fold
            wbuf[c][1][plane] = jnp.concatenate(
                [piece[q * part : (q + 1) * part, main:] for q in range(fold)], axis=1
            ).astype(BF16)

    def relay(zz, c, up):
        target = (plane + 1 if up else plane - 1) * GROUP + member
        way = 1 if up else 0
        return [
            remote(
                ref.at[zz], ref.at[zz], s_z.at[way, zz, c * per + q], r_z.at[zz, c * per + q],
                target, tp,
            )
            for q, ref in enumerate(wbuf[c])
        ]

    def pass_on(zz, c, act):
        @pl.when((zz <= plane) & (plane + 1 < planes))
        def _():
            for copy in relay(zz, c, True):
                act(copy)

        @pl.when((zz >= plane) & (plane > 0))
        def _():
            for copy in relay(zz, c, False):
                act(copy)

    def take_and_pass(far, c):
        @pl.loop(0, 2)
        def _(side):
            zz = plane + (2 * side - 1) * far

            @pl.when((zz >= 0) & (zz < planes))
            def _():
                for copy in relay(zz, c, True):
                    copy.wait_recv()
                pass_on(zz, c, lambda copy: copy.start())

    for c in range(nchunks):
        pass_on(plane, c, lambda copy: copy.start())

    for other_tp in range(ntp):
        @pl.when(other_tp != tp)
        def _():
            stats_copy(other_tp, other_tp).wait_recv()
    columns = jnp.concatenate(
        [vec_ref[:, q * feats : (q + 1) * feats] for q in range(3)] + [jnp.zeros((5, feats), F32)],
        axis=0,
    ).T
    gain, bias = columns[:, 0:1], columns[:, 1:2]
    mcol[...] = jnp.broadcast_to(columns[:, 2:3], (feats, LANES))
    wide = GROUP * LANES
    from_tok = lax.broadcasted_iota(jnp.int32, (wide, wide), 0)
    to_tok = lax.broadcasted_iota(jnp.int32, (wide, wide), 1)
    sorter = (from_tok == GROUP * (to_tok % LANES) + to_tok // LANES).astype(F32).astype(BF16)
    for c in range(tokens // wide):
        at = slice(c * wide, (c + 1) * wide)
        mean = sum(stats[q, 0:1, at] for q in range(ntp)) / ntp
        square = sum(
            stats[q, 1:2, at] + feats * (stats[q, 0:1, at] - mean) ** 2 for q in range(ntp)
        )
        scale = lax.rsqrt(square / (feats * ntp) + 1e-06)
        normed = (
            (x_ref[:, at].astype(F32) - mean) * scale * gain + bias
        ).astype(BF16)
        by_patch = jnp.dot(normed, sorter, preferred_element_type=F32).astype(BF16)
        for i in range(GROUP):
            xs[i, :, c * LANES : (c + 1) * LANES] = by_patch[:, i * LANES : (i + 1) * LANES]

    def token_copy(i, slot, sem):
        return remote(xs.at[i], tok.at[slot], s_t.at[i], r_t.at[sem], plane * GROUP + i, tp)

    for i in range(GROUP):
        @pl.when(i != member)
        def _():
            token_copy(i, member, member).start()
    tok[member] = xs[member]

    def core_copy(zz, c):
        home = zz // owned
        at = pl.ds(*chunks[c])
        return remote(
            psend.at[zz, :, at], cores.at[zz - home * owned, tp, :, at],
            s_c.at[zz, c], r_c.at[zz - home * owned, c, tp], me, home,
        )

    def part_copy(b, c, i):
        at = pl.ds(*chunks[c])
        return remote(
            summed.at[b, i, at], parts.at[b, member, at],
            s_p.at[b, c, i], r_p.at[b, c, member], plane * GROUP + i, tp,
        )

    def use_chunk(zz, c):
        at = pl.ds(*chunks[c])
        weight = wbuf[c][0][zz]
        if fold:
            lanes = LANES // fold
            rest = wbuf[c][1][zz]
            rest = jnp.concatenate(
                [rest[:, q * lanes : (q + 1) * lanes] for q in range(fold)], axis=0
            )
            weight = jnp.concatenate([weight, rest], axis=1)
        for i in range(GROUP):
            psend[zz, i, at] = contract(weight, tok[i], 1, 0).astype(BF16)

        @pl.when(zz // owned != tp)
        def _():
            core_copy(zz, c).start()

    def join_chunk(zz, c):
        b = zz - tp * owned
        at = pl.ds(*chunks[c])
        for q in range(ntp):
            @pl.when(q != tp)
            def _():
                remote(
                    psend.at[zz, :, at], cores.at[b, q, :, at], s_c.at[zz, c], r_c.at[b, c, q], me, q
                ).wait_recv()

            @pl.when(q == tp)
            def _():
                cores[b, q, :, at] = psend[zz, :, at]
        for i in range(GROUP):
            total = sum(cores[b, q, i, at].astype(F32) for q in range(ntp))
            summed[b, i, at] = total.astype(BF16)

            @pl.when(i != member)
            def _():
                part_copy(b, c, i).start()

            @pl.when(i == member)
            def _():
                parts[b, member, at] = summed[b, i, at]

    def row_copy(b, c, other, slot):
        return remote(
            send[c].at[b, other], got[c].at[b, slot],
            s_d.at[b, c, other], r_d.at[b, c, slot], other, tp,
        )

    def place_chunk(zz, c):
        b = zz - tp * owned
        row0, size = chunks[c]
        at = pl.ds(row0, size)
        total = jnp.zeros((size, rows), F32)
        for i in range(GROUP):
            @pl.when(i != member)
            def _():
                remote(
                    summed.at[b, i, at], parts.at[b, i, at],
                    s_p.at[b, c, i], r_p.at[b, c, i], plane * GROUP + i, tp,
                ).wait_recv()
            total = total + parts[b, i, at].astype(F32)
        shift = mcol[pl.ds(pl.multiple_of(b * block_cols + row0, 8), size), :][:, 0:1]
        merged = (total + shift).T.astype(BF16)

        @pl.loop(0, planes)
        def _(step):
            to = lax.rem(plane + planes // 2 + step, planes)
            picked = contract(pick[to], merged, 1, 0)
            for i in range(GROUP):
                other = to * GROUP + i
                send[c][b, other] = pack_rows(
                    picked[i * slots : (i + 1) * slots], slots, size
                ).astype(BF16)

                @pl.when(other != me)
                def _():
                    row_copy(b, c, other, me).start()

                @pl.when(other == me)
                def _():
                    got[c][b, me] = send[c][b, me]

    def both_sides(far, act):
        @pl.loop(0, 2)
        def _(side):
            zz = plane + (2 * side - 1) * far

            @pl.when((zz >= 0) & (zz < planes) & ((far > 0) | (side == 0)))
            def _():
                act(zz)

    def owned_sides(far, c, act):
        def act_owned(zz):
            @pl.when(zz // owned == tp)
            def _():
                act(zz, c)

        both_sides(far, act_owned)

    take_and_pass(1, 0)

    trow = trow_ref[...]
    tcol = jnp.broadcast_to(trow.astype(F32), (8, rows)).T[:, 0:1].astype(jnp.int32)
    dest_row = trow // prompt_rows
    dest_col = tcol // prompt_rows
    first = lax.broadcasted_iota(jnp.int32, (rows, rows), 0)
    second = lax.broadcasted_iota(jnp.int32, (rows, rows), 1)
    same = dest_col == dest_row
    order_row = jnp.sum((same & (first < second)).astype(F32), axis=0, keepdims=True)
    order_col = jnp.sum((same & (second < first)).astype(F32), axis=1, keepdims=True)
    slot_row = dest_row * slots + order_row.astype(jnp.int32)
    slot_col = dest_col * slots + order_col.astype(jnp.int32)
    local_col = (tcol - dest_col * prompt_rows + 1).astype(F32)

    @pl.loop(0, planes)
    def _(to):
        size = GROUP * slots
        slot_at = to * size + lax.broadcasted_iota(jnp.int32, (size, rows), 0)
        pick[to] = (slot_at == slot_row).astype(F32).astype(BF16)

    for c in range(1, nchunks):
        take_and_pass(1, c)

    def pos_copy(other, slot):
        return remote(
            posend.at[other], posbuf.at[slot], s_pos.at[other], r_pos.at[slot], other, tp
        )

    @pl.loop(0, nseq)
    def _(other):
        base = other * slots
        lane = lax.broadcasted_iota(jnp.int32, (rows, LANES), 1)
        held = jnp.where((slot_col == base + lane) & (lane < slots), local_col, 0.0)
        posend[other] = jnp.broadcast_to(jnp.sum(held, axis=0, keepdims=True), (8, LANES))

        @pl.when(other != me)
        def _():
            pos_copy(other, me).start()

        @pl.when(other == me)
        def _():
            posbuf[me] = posend[me]

    if planes > 3:
        take_and_pass(2, 0)
    for i in range(GROUP):
        @pl.when(i != member)
        def _():
            token_copy(i, i, i).wait_recv()
    for c in range(nchunks):
        use_chunk(plane, c)
    if planes > 3:
        for c in range(1, nchunks):
            take_and_pass(2, c)

    @pl.loop(3, max(planes - 1, 3))
    def _(far):
        for c in range(nchunks):
            take_and_pass(far, c)

    @pl.loop(0, planes)
    def _(far):
        for c in range(nchunks):
            @pl.when((far > 1) & (far == planes - 1))
            def _():
                take_and_pass(far, c)

            @pl.when(far > 0)
            def _():
                both_sides(far, lambda zz: use_chunk(zz, c))
            if c:
                owned_sides(far, c - 1, place_chunk)
            else:
                @pl.when(far > 0)
                def _():
                    owned_sides(far - 1, nchunks - 1, place_chunk)
            owned_sides(far, c, join_chunk)

    diagonal = lax.broadcasted_iota(jnp.int32, (slots, LANES), 0) == lax.broadcasted_iota(
        jnp.int32, (slots, LANES), 1
    )
    position = (
        lax.broadcasted_iota(jnp.int32, (GROUP * slots, prompt_rows), 1).astype(F32) + 1.0
    )

    def spots(source, hits):
        lines = []
        for i in range(GROUP):
            other = source * GROUP + i

            @pl.when(other != me)
            def _():
                pos_copy(other, other).wait_recv()
            line = posbuf[other][0:1]
            lines.append(jnp.sum(jnp.where(diagonal, line, 0.0), axis=1, keepdims=True))
        spot = (jnp.concatenate(lines, axis=0) == position).astype(F32)
        place[source] = spot.astype(BF16)
        return hits + jnp.sum(spot, axis=0, keepdims=True)

    hits = lax.fori_loop(0, planes, spots, jnp.zeros((1, prompt_rows), F32))
    owned_sides(planes - 1, nchunks - 1, place_chunk)

    for b in range(owned):
        for c, (row0, size) in enumerate(chunks):
            @pl.loop(0, nseq)
            def _(other):
                @pl.when(other != me)
                def _():
                    row_copy(b, c, other, other).wait_recv()
            arrived = jnp.concatenate(
                [unpack_rows(got[c][b, s].astype(F32), slots, size) for s in range(nseq)], axis=0
            ).astype(BF16)
            image = contract(arrived, place[...].reshape(nseq * slots, prompt_rows), 0, 0)
            at = slice(b * block_cols + row0, b * block_cols + row0 + size)
            out_ref[at, :] = jnp.where(hits > 0.5, image.astype(BF16), text_ref[at, :])

    for i in range(GROUP):
        @pl.when(i != member)
        def _():
            weight_copy(i).wait_send()
            token_copy(i, member, member).wait_send()
    for other_tp in range(ntp):
        @pl.when(other_tp != tp)
        def _():
            stats_copy(other_tp, tp).wait_send()

    @pl.loop(0, planes)
    def _(zz):
        for c in range(nchunks):
            pass_on(zz, c, lambda copy: copy.wait_send())

            @pl.when(zz // owned != tp)
            def _():
                core_copy(zz, c).wait_send()

            @pl.when(zz // owned == tp)
            def _():
                for i in range(GROUP):
                    @pl.when(i != member)
                    def _():
                        part_copy(zz - tp * owned, c, i).wait_send()

    @pl.loop(0, nseq)
    def _(other):
        @pl.when(other != me)
        def _():
            pos_copy(other, me).wait_send()
            for b in range(owned):
                for c in range(nchunks):
                    row_copy(b, c, other, me).wait_send()


def shards(patches, ln_gain, ln_bias, merge_weight, merge_bias, targets, text_embed):
    nseq, ntp = lax.axis_size("seq"), lax.axis_size("tp")
    feats, tokens = patches.shape
    rows = tokens // GROUP
    shard_cols = merge_weight.shape[2]
    planes = nseq // GROUP
    owned = planes // ntp
    block_cols = GROUP * shard_cols
    prompt_rows = text_embed.shape[1]
    slots = round_up(5 * rows // (2 * nseq), 8)
    chunks = chunks_of(block_cols)
    main, fold = folding(feats, block_cols)
    pieces = []
    for _, size in chunks:
        pieces.append(pltpu.VMEM((planes, size, main), BF16))
        if fold:
            pieces.append(pltpu.VMEM((planes, size // fold, LANES), BF16))
    payloads = [
        pltpu.VMEM((owned, nseq, payload_rows(slots, size), LANES), BF16)
        for _, size in chunks
    ]
    dma = pltpu.SemaphoreType.DMA
    count = len(chunks)
    return pl.pallas_call(
        functools.partial(merge_kernel, nseq, ntp, slots, len(pieces), count),
        out_shape=jax.ShapeDtypeStruct(text_embed.shape, text_embed.dtype),
        in_specs=[pl.BlockSpec(memory_space=pltpu.VMEM)] * 5,
        out_specs=pl.BlockSpec(memory_space=pltpu.VMEM),
        scratch_shapes=[
            pltpu.VMEM((ntp, 2, tokens), F32),
            pltpu.VMEM((GROUP, feats, rows), BF16),
            pltpu.VMEM((GROUP, feats, rows), BF16),
            pltpu.VMEM((GROUP, shard_cols, feats), BF16),
            pltpu.VMEM((planes, GROUP, block_cols, rows), BF16),
            pltpu.VMEM((owned, ntp, GROUP, block_cols, rows), BF16),
            pltpu.VMEM((owned, GROUP, block_cols, rows), BF16),
            pltpu.VMEM((owned, GROUP, block_cols, rows), BF16),
            pltpu.VMEM((feats, LANES), F32),
            pltpu.VMEM((planes, GROUP * slots, rows), BF16),
            pltpu.VMEM((nseq, 8, LANES), F32),
            pltpu.VMEM((nseq, 8, LANES), F32),
            pltpu.VMEM((planes, GROUP * slots, prompt_rows), BF16),
            dma((GROUP,)), dma((GROUP,)),
            dma((2, planes, len(pieces))), dma((planes, len(pieces))),
            dma((GROUP,)), dma((GROUP,)),
            dma((ntp,)), dma((ntp,)),
            dma((planes, count)), dma((owned, count, ntp)),
            dma((owned, count, GROUP)), dma((owned, count, GROUP)),
            dma((owned, count, nseq)), dma((owned, count, nseq)),
            dma((nseq,)), dma((nseq,)),
        ] + pieces + payloads + payloads,
        compiler_params=pltpu.CompilerParams(
            collective_id=0, has_side_effects=True, vmem_limit_bytes=56 * 2**20
        ),
    )(
        patches,
        jnp.concatenate([v.astype(F32) for v in (ln_gain, ln_bias, merge_bias)])[None, :],
        jnp.swapaxes(merge_weight, 1, 2),
        targets[None, :],
        text_embed,
    )


def solution(mesh):
    in_specs = (
        P("tp", "seq"),
        P("tp"),
        P("tp"),
        P(None, "tp", "seq"),
        P("tp"),
        P("seq"),
        P("tp", "seq"),
    )
    out_specs = P("tp", "seq")
    return jax.shard_map(shards, mesh=mesh, in_specs=in_specs, out_specs=out_specs, check_vma=False)
```

```python
import functools

import jax
import jax.numpy as jnp
from jax import lax
from jax.experimental import pallas as pl
from jax.experimental.pallas import tpu as pltpu
from jax.sharding import PartitionSpec as P

D = 1664
GROUP = 4
LANES = 128
MESH = pl.DeviceIdType.MESH
F32 = jnp.float32
BF16 = jnp.bfloat16


def contract(lhs, rhs, lhs_dim, rhs_dim):
    return lax.dot_general(
        lhs, rhs, (((lhs_dim,), (rhs_dim,)), ((), ())), preferred_element_type=F32
    )


def round_up(value, unit):
    return -(-value // unit) * unit


def split_columns(feats, shard_cols):
    main = feats // LANES * LANES
    rest = feats - main
    if main and rest and LANES % rest == 0 and shard_cols > 64:
        fold = LANES // rest
        sizes = [64, shard_cols - 64]
        if all(GROUP * size % (16 * fold) == 0 and size % 8 == 0 for size in sizes) and 64 % (16 * fold) == 0:
            return sizes, main, fold
    return [shard_cols], feats, 0


def payload_rows(slots, size):
    full, rest = divmod(size, LANES)
    total = full * slots
    if rest:
        fold = LANES // rest if LANES % rest == 0 else 1
        total += 8 * (-(-(slots // 8) // fold))
    return round_up(total, 16)


def pack_rows(rows, slots, size):
    full, rest = divmod(size, LANES)
    parts = [rows[:, q * LANES : (q + 1) * LANES] for q in range(full)]
    if rest:
        fold = LANES // rest if LANES % rest == 0 else 1
        groups = [rows[8 * g : 8 * g + 8, full * LANES :] for g in range(slots // 8)]
        for g in range(0, len(groups), fold):
            line = groups[g : g + fold]
            short = LANES - rest * len(line)
            if short:
                line = line + [jnp.zeros((8, short), F32)]
            parts.append(jnp.concatenate(line, axis=1))
    have = sum(part.shape[0] for part in parts)
    if have < payload_rows(slots, size):
        parts.append(jnp.zeros((payload_rows(slots, size) - have, LANES), F32))
    return jnp.concatenate(parts, axis=0)


def unpack_rows(stack, slots, size):
    full, rest = divmod(size, LANES)
    parts = [stack[q * slots : (q + 1) * slots] for q in range(full)]
    if rest:
        fold = LANES // rest if LANES % rest == 0 else 1
        base = full * slots
        groups = []
        for g in range(slots // 8):
            line = base + 8 * (g // fold)
            lane = (g % fold) * rest
            groups.append(stack[line : line + 8, lane : lane + rest])
        parts.append(jnp.concatenate(groups, axis=0))
    return jnp.concatenate(parts, axis=1)


def merge_kernel(
    nseq, ntp, slots, npieces, nchunks,
    x_ref, vec_ref, w_ref, trow_ref, text_ref,
    out_ref,
    stats, xs, tok, w_low, wpl0, wpl1, psend, cores, summed, parts, mcol, pick, posend, posbuf, place,
    s_w, r_w, s_z, r_z, s_t, r_t, s_st, r_st, s_c, r_c, s_p, r_p, s_d, r_d, s_pos, r_pos,
    *buffers,
):
    me, tp = lax.axis_index("seq"), lax.axis_index("tp")
    plane, member = me // GROUP, lax.rem(me, GROUP)
    planes = nseq // GROUP
    owned = planes // ntp
    feats, tokens = x_ref.shape
    rows = tokens // GROUP
    prompt_rows = text_ref.shape[1]
    shard_cols = w_ref.shape[1]
    block_cols = shard_cols * GROUP
    sizes, main, fold = split_columns(feats, shard_cols)
    chunks = []
    for size in sizes:
        chunks.append((sum(n for _, n in chunks), GROUP * size))
    per = 2 if fold else 1
    wbuf = [buffers[c * per : (c + 1) * per] for c in range(nchunks)]
    send = buffers[npieces : npieces + nchunks]
    got = buffers[npieces + nchunks :]

    def remote(src, dst, send_sem, recv_sem, seq_id, tp_id):
        return pltpu.make_async_remote_copy(
            src_ref=src, dst_ref=dst, send_sem=send_sem, recv_sem=recv_sem,
            device_id=(seq_id, tp_id), device_id_type=MESH,
        )

    barrier = pltpu.get_barrier_semaphore()

    @pl.loop(0, nseq)
    def _(other):
        @pl.when(other != me)
        def _():
            pl.semaphore_signal(barrier, inc=1, device_id=(other, tp), device_id_type=MESH)

    for other_tp in range(ntp):
        @pl.when(other_tp != tp)
        def _():
            for i in range(GROUP):
                pl.semaphore_signal(
                    barrier, inc=1, device_id=(plane * GROUP + i, other_tp), device_id_type=MESH
                )
    pl.semaphore_wait(barrier, nseq - 1 + GROUP * (ntp - 1))

    first_cols = sizes[0]

    def weight_copy(i, c, slot):
        if c:
            src, dst = w_low.at[i], wpl1.at[slot]
        else:
            src = w_ref.at[i, pl.ds(0, first_cols)] if nchunks > 1 else w_ref.at[i]
            dst = wpl0.at[slot]
        return remote(src, dst, s_w.at[c, i], r_w.at[c, slot], plane * GROUP + i, tp)

    def send_weight(c):
        for i in range(GROUP):
            @pl.when(i != member)
            def _():
                weight_copy(i, c, member).start()

    def wait_weight(c):
        for i in range(GROUP):
            @pl.when(i != member)
            def _():
                weight_copy(i, c, i).wait_recv()

    def fold_lanes(rows_in):
        part = rows_in.shape[0] // fold
        return jnp.concatenate(
            [rows_in[q * part : (q + 1) * part, main:] for q in range(fold)], axis=1
        ).astype(BF16)

    def unfold_lanes(folded):
        lanes = LANES // fold
        return jnp.concatenate(
            [folded[:, q * lanes : (q + 1) * lanes] for q in range(fold)], axis=0
        )

    def put_first(slot, rows_in):
        wbuf[0][0][plane, slot] = rows_in[:, :main]
        if fold:
            wbuf[0][1][plane, slot] = fold_lanes(rows_in)

    moves = 2 + (nchunks - 1)

    def relay(zz, move, up):
        target = (plane + 1 if up else plane - 1) * GROUP + member
        way = 1 if up else 0
        copies = []
        for q, ref in enumerate(wbuf[move // 2]):
            view = (ref.at[zz, 0], ref.at[zz, pl.ds(1, GROUP - 1)], ref.at[zz])[move]
            copies.append(
                remote(
                    view, view, s_z.at[way, zz, move * per + q], r_z.at[zz, move * per + q],
                    target, tp,
                )
            )
        return copies

    def pass_on(zz, move, act):
        @pl.when((zz <= plane) & (plane + 1 < planes))
        def _():
            for copy in relay(zz, move, True):
                act(copy)

        @pl.when((zz >= plane) & (plane > 0))
        def _():
            for copy in relay(zz, move, False):
                act(copy)

    def take_and_pass(far, move):
        @pl.loop(0, 2)
        def _(side):
            zz = plane + (2 * side - 1) * far

            @pl.when((zz >= 0) & (zz < planes))
            def _():
                for copy in relay(zz, move, True):
                    copy.wait_recv()
                pass_on(zz, move, lambda copy: copy.start())

    send_weight(0)
    put_first(0, w_ref[member][:first_cols])
    pass_on(plane, 0, lambda copy: copy.start())
    if nchunks > 1:
        for i in range(GROUP):
            w_low[i, 0 : sizes[1]] = w_ref[i, first_cols:]
            if w_low.shape[1] > sizes[1]:
                w_low[i, sizes[1] :] = jnp.zeros((w_low.shape[1] - sizes[1], feats), BF16)
        send_weight(1)

    chunk = 256

    @pl.loop(0, tokens // chunk)
    def _(c):
        at = pl.ds(pl.multiple_of(c * chunk, chunk), chunk)
        values = x_ref[:, at].astype(F32)
        mean = jnp.sum(values, axis=0, keepdims=True) / feats
        apart = values - mean
        stats[tp, 0:1, at] = mean
        stats[tp, 1:2, at] = jnp.sum(apart * apart, axis=0, keepdims=True)

    def stats_copy(other_tp, slot):
        return remote(
            stats.at[slot], stats.at[slot], s_st.at[other_tp], r_st.at[slot], me, other_tp
        )

    for other_tp in range(ntp):
        @pl.when(other_tp != tp)
        def _():
            stats_copy(other_tp, tp).start()

    wait_weight(0)
    for r in range(1, GROUP):
        put_first(r, wpl0[lax.rem(member + r, GROUP)])
    pass_on(plane, 1, lambda copy: copy.start())
    for other_tp in range(ntp):
        @pl.when(other_tp != tp)
        def _():
            stats_copy(other_tp, other_tp).wait_recv()
    columns = jnp.concatenate(
        [vec_ref[:, q * feats : (q + 1) * feats] for q in range(3)] + [jnp.zeros((5, feats), F32)],
        axis=0,
    ).T
    gain, bias = columns[:, 0:1], columns[:, 1:2]
    for b in range(owned):
        for c, (row0, size) in enumerate(chunks):
            for i in range(GROUP):
                come = b * block_cols + i * shard_cols + sum(sizes[:c])
                go = b * block_cols + row0 + i * sizes[c]
                mcol[go : go + sizes[c]] = jnp.broadcast_to(
                    columns[come : come + sizes[c], 2:3], (sizes[c], LANES)
                )
    wide = GROUP * LANES
    from_tok = lax.broadcasted_iota(jnp.int32, (wide, wide), 0)
    to_tok = lax.broadcasted_iota(jnp.int32, (wide, wide), 1)
    sorter = (from_tok == GROUP * (to_tok % LANES) + to_tok // LANES).astype(F32).astype(BF16)
    for c in range(tokens // wide):
        at = slice(c * wide, (c + 1) * wide)
        mean = sum(stats[q, 0:1, at] for q in range(ntp)) / ntp
        square = sum(
            stats[q, 1:2, at] + feats * (stats[q, 0:1, at] - mean) ** 2 for q in range(ntp)
        )
        scale = lax.rsqrt(square / (feats * ntp) + 1e-06)
        normed = (
            (x_ref[:, at].astype(F32) - mean) * scale * gain + bias
        ).astype(BF16)
        by_patch = jnp.dot(normed, sorter, preferred_element_type=F32).astype(BF16)
        for i in range(GROUP):
            xs[i, :, c * LANES : (c + 1) * LANES] = by_patch[:, i * LANES : (i + 1) * LANES]

    def token_copy(i, slot, sem):
        return remote(xs.at[i], tok.at[slot], s_t.at[i], r_t.at[sem], plane * GROUP + i, tp)

    for i in range(GROUP):
        @pl.when(i != member)
        def _():
            token_copy(i, member, member).start()
    tok[member] = xs[member]

    if nchunks > 1:
        wait_weight(1)
        wpl1[member] = w_low[member]
        low = jnp.concatenate(
            [wpl1[i].astype(F32)[: sizes[1]] for i in range(GROUP)], axis=0
        )
        wbuf[1][0][plane] = low[:, :main].astype(BF16)
        wbuf[1][1][plane] = fold_lanes(low)
        pass_on(plane, 2, lambda copy: copy.start())

    def core_copy(zz, c):
        home = zz // owned
        at = pl.ds(*chunks[c])
        return remote(
            psend.at[zz, :, at], cores.at[zz - home * owned, tp, :, at],
            s_c.at[zz, c], r_c.at[zz - home * owned, c, tp], me, home,
        )

    def part_copy(b, c, i):
        at = pl.ds(*chunks[c])
        return remote(
            summed.at[b, i, at], parts.at[b, member, at],
            s_p.at[b, c, i], r_p.at[b, c, member], plane * GROUP + i, tp,
        )

    def use_chunk(zz, c):
        at = pl.ds(*chunks[c])
        if c:
            weight = jnp.concatenate([wbuf[1][0][zz], unfold_lanes(wbuf[1][1][zz])], axis=1)
        else:
            members = []
            for i in range(GROUP):
                slot = lax.rem(i - member + GROUP, GROUP)
                piece = wbuf[0][0][zz, slot]
                if fold:
                    piece = jnp.concatenate([piece, unfold_lanes(wbuf[0][1][zz, slot])], axis=1)
                members.append(piece if fold else piece.astype(F32))
            weight = jnp.concatenate(members, axis=0).astype(BF16)
        for i in range(GROUP):
            psend[zz, i, at] = contract(weight, tok[i], 1, 0).astype(BF16)

        @pl.when(zz // owned != tp)
        def _():
            core_copy(zz, c).start()

    def join_chunk(zz, c):
        b = zz - tp * owned
        at = pl.ds(*chunks[c])
        for q in range(ntp):
            @pl.when(q != tp)
            def _():
                remote(
                    psend.at[zz, :, at], cores.at[b, q, :, at], s_c.at[zz, c], r_c.at[b, c, q], me, q
                ).wait_recv()

            @pl.when(q == tp)
            def _():
                cores[b, q, :, at] = psend[zz, :, at]
        for i in range(GROUP):
            total = sum(cores[b, q, i, at].astype(F32) for q in range(ntp))
            summed[b, i, at] = total.astype(BF16)

            @pl.when(i != member)
            def _():
                part_copy(b, c, i).start()

            @pl.when(i == member)
            def _():
                parts[b, member, at] = summed[b, i, at]

    def row_copy(b, c, other, slot):
        return remote(
            send[c].at[b, other], got[c].at[b, slot],
            s_d.at[b, c, other], r_d.at[b, c, slot], other, tp,
        )

    def place_chunk(zz, c):
        b = zz - tp * owned
        row0, size = chunks[c]
        at = pl.ds(row0, size)
        total = jnp.zeros((size, rows), F32)
        for i in range(GROUP):
            @pl.when(i != member)
            def _():
                remote(
                    summed.at[b, i, at], parts.at[b, i, at],
                    s_p.at[b, c, i], r_p.at[b, c, i], plane * GROUP + i, tp,
                ).wait_recv()
            total = total + parts[b, i, at].astype(F32)
        shift = mcol[pl.ds(pl.multiple_of(b * block_cols + row0, 8), size), :][:, 0:1]
        merged = (total + shift).T.astype(BF16)

        @pl.loop(0, planes)
        def _(step):
            to = lax.rem(plane + planes // 2 + step, planes)
            picked = contract(pick[to], merged, 1, 0)
            for i in range(GROUP):
                other = to * GROUP + i
                send[c][b, other] = pack_rows(
                    picked[i * slots : (i + 1) * slots], slots, size
                ).astype(BF16)

                @pl.when(other != me)
                def _():
                    row_copy(b, c, other, me).start()

                @pl.when(other == me)
                def _():
                    got[c][b, me] = send[c][b, me]

    def both_sides(far, act):
        @pl.loop(0, 2)
        def _(side):
            zz = plane + (2 * side - 1) * far

            @pl.when((zz >= 0) & (zz < planes) & ((far > 0) | (side == 0)))
            def _():
                act(zz)

    def owned_sides(far, c, act):
        def act_owned(zz):
            @pl.when(zz // owned == tp)
            def _():
                act(zz, c)

        both_sides(far, act_owned)

    take_and_pass(1, 0)
    take_and_pass(1, 1)

    trow = trow_ref[...]
    tcol = jnp.broadcast_to(trow.astype(F32), (8, rows)).T[:, 0:1].astype(jnp.int32)
    dest_row = trow // prompt_rows
    dest_col = tcol // prompt_rows
    first = lax.broadcasted_iota(jnp.int32, (rows, rows), 0)
    second = lax.broadcasted_iota(jnp.int32, (rows, rows), 1)
    same = dest_col == dest_row
    order_row = jnp.sum((same & (first < second)).astype(F32), axis=0, keepdims=True)
    order_col = jnp.sum((same & (second < first)).astype(F32), axis=1, keepdims=True)
    slot_row = dest_row * slots + order_row.astype(jnp.int32)
    slot_col = dest_col * slots + order_col.astype(jnp.int32)
    local_col = (tcol - dest_col * prompt_rows + 1).astype(F32)

    @pl.loop(0, planes)
    def _(to):
        size = GROUP * slots
        slot_at = to * size + lax.broadcasted_iota(jnp.int32, (size, rows), 0)
        pick[to] = (slot_at == slot_row).astype(F32).astype(BF16)

    if moves > 2:
        take_and_pass(1, 2)

    def pos_copy(other, slot):
        return remote(
            posend.at[other], posbuf.at[slot], s_pos.at[other], r_pos.at[slot], other, tp
        )

    @pl.loop(0, nseq)
    def _(other):
        base = other * slots
        lane = lax.broadcasted_iota(jnp.int32, (rows, LANES), 1)
        held = jnp.where((slot_col == base + lane) & (lane < slots), local_col, 0.0)
        posend[other] = jnp.broadcast_to(jnp.sum(held, axis=0, keepdims=True), (8, LANES))

        @pl.when(other != me)
        def _():
            pos_copy(other, me).start()

        @pl.when(other == me)
        def _():
            posbuf[me] = posend[me]

    for i in range(GROUP):
        @pl.when(i != member)
        def _():
            token_copy(i, i, i).wait_recv()

    @pl.loop(0, planes)
    def _(far):
        for c in range(nchunks):
            @pl.when(far > 1)
            def _():
                for move in (2,) if c else (0, 1):
                    take_and_pass(far, move)
            both_sides(far, lambda zz: use_chunk(zz, c))
            if c:
                owned_sides(far, c - 1, place_chunk)
            else:
                @pl.when(far > 0)
                def _():
                    owned_sides(far - 1, nchunks - 1, place_chunk)
            owned_sides(far, c, join_chunk)

    diagonal = lax.broadcasted_iota(jnp.int32, (slots, LANES), 0) == lax.broadcasted_iota(
        jnp.int32, (slots, LANES), 1
    )
    position = (
        lax.broadcasted_iota(jnp.int32, (GROUP * slots, prompt_rows), 1).astype(F32) + 1.0
    )

    def spots(source, hits):
        lines = []
        for i in range(GROUP):
            other = source * GROUP + i

            @pl.when(other != me)
            def _():
                pos_copy(other, other).wait_recv()
            line = posbuf[other][0:1]
            lines.append(jnp.sum(jnp.where(diagonal, line, 0.0), axis=1, keepdims=True))
        spot = (jnp.concatenate(lines, axis=0) == position).astype(F32)
        place[source] = spot.astype(BF16)
        return hits + jnp.sum(spot, axis=0, keepdims=True)

    hits = lax.fori_loop(0, planes, spots, jnp.zeros((1, prompt_rows), F32))
    owned_sides(planes - 1, nchunks - 1, place_chunk)

    for b in range(owned):
        images = []
        for c, (row0, size) in enumerate(chunks):
            @pl.loop(0, nseq)
            def _(other):
                @pl.when(other != me)
                def _():
                    row_copy(b, c, other, other).wait_recv()
            arrived = jnp.concatenate(
                [unpack_rows(got[c][b, s].astype(F32), slots, size) for s in range(nseq)], axis=0
            ).astype(BF16)
            images.append(
                contract(arrived, place[...].reshape(nseq * slots, prompt_rows), 0, 0)
            )
        image = jnp.concatenate(
            [
                images[c][i * sizes[c] : (i + 1) * sizes[c]]
                for i in range(GROUP)
                for c in range(nchunks)
            ],
            axis=0,
        )
        at = slice(b * block_cols, (b + 1) * block_cols)
        out_ref[at, :] = jnp.where(hits > 0.5, image.astype(BF16), text_ref[at, :])

    for i in range(GROUP):
        @pl.when(i != member)
        def _():
            for c in range(nchunks):
                weight_copy(i, c, member).wait_send()
            token_copy(i, member, member).wait_send()
    for other_tp in range(ntp):
        @pl.when(other_tp != tp)
        def _():
            stats_copy(other_tp, tp).wait_send()

    @pl.loop(0, planes)
    def _(zz):
        for move in range(moves):
            pass_on(zz, move, lambda copy: copy.wait_send())
        for c in range(nchunks):

            @pl.when(zz // owned != tp)
            def _():
                core_copy(zz, c).wait_send()

            @pl.when(zz // owned == tp)
            def _():
                for i in range(GROUP):
                    @pl.when(i != member)
                    def _():
                        part_copy(zz - tp * owned, c, i).wait_send()

    @pl.loop(0, nseq)
    def _(other):
        @pl.when(other != me)
        def _():
            pos_copy(other, me).wait_send()
            for b in range(owned):
                for c in range(nchunks):
                    row_copy(b, c, other, me).wait_send()


def shards(patches, ln_gain, ln_bias, merge_weight, merge_bias, targets, text_embed):
    nseq, ntp = lax.axis_size("seq"), lax.axis_size("tp")
    feats, tokens = patches.shape
    rows = tokens // GROUP
    shard_cols = merge_weight.shape[2]
    planes = nseq // GROUP
    owned = planes // ntp
    block_cols = GROUP * shard_cols
    prompt_rows = text_embed.shape[1]
    slots = round_up(5 * rows // (2 * nseq), 8)
    sizes, main, fold = split_columns(feats, shard_cols)
    chunks = [(0, GROUP * size) for size in sizes]
    low_rows = round_up(sizes[-1], 16)
    pieces = [pltpu.VMEM((planes, GROUP, sizes[0], main), BF16)]
    if fold:
        pieces += [
            pltpu.VMEM((planes, GROUP, sizes[0] // fold, LANES), BF16),
            pltpu.VMEM((planes, GROUP * sizes[1], main), BF16),
            pltpu.VMEM((planes, GROUP * sizes[1] // fold, LANES), BF16),
        ]
    payloads = [
        pltpu.VMEM((owned, nseq, payload_rows(slots, size), LANES), BF16)
        for _, size in chunks
    ]
    dma = pltpu.SemaphoreType.DMA
    count = len(chunks)
    return pl.pallas_call(
        functools.partial(merge_kernel, nseq, ntp, slots, len(pieces), count),
        out_shape=jax.ShapeDtypeStruct(text_embed.shape, text_embed.dtype),
        in_specs=[pl.BlockSpec(memory_space=pltpu.VMEM)] * 5,
        out_specs=pl.BlockSpec(memory_space=pltpu.VMEM),
        scratch_shapes=[
            pltpu.VMEM((ntp, 2, tokens), F32),
            pltpu.VMEM((GROUP, feats, rows), BF16),
            pltpu.VMEM((GROUP, feats, rows), BF16),
            pltpu.VMEM((GROUP, low_rows, feats), BF16),
            pltpu.VMEM((GROUP, sizes[0], feats), BF16),
            pltpu.VMEM((GROUP, low_rows, feats), BF16),
            pltpu.VMEM((planes, GROUP, block_cols, rows), BF16),
            pltpu.VMEM((owned, ntp, GROUP, block_cols, rows), BF16),
            pltpu.VMEM((owned, GROUP, block_cols, rows), BF16),
            pltpu.VMEM((owned, GROUP, block_cols, rows), BF16),
            pltpu.VMEM((feats, LANES), F32),
            pltpu.VMEM((planes, GROUP * slots, rows), BF16),
            pltpu.VMEM((nseq, 8, LANES), F32),
            pltpu.VMEM((nseq, 8, LANES), F32),
            pltpu.VMEM((planes, GROUP * slots, prompt_rows), BF16),
            dma((2, GROUP)), dma((2, GROUP)),
            dma((2, planes, 6)), dma((planes, 6)),
            dma((GROUP,)), dma((GROUP,)),
            dma((ntp,)), dma((ntp,)),
            dma((planes, count)), dma((owned, count, ntp)),
            dma((owned, count, GROUP)), dma((owned, count, GROUP)),
            dma((owned, count, nseq)), dma((owned, count, nseq)),
            dma((nseq,)), dma((nseq,)),
        ] + pieces + payloads + payloads,
        compiler_params=pltpu.CompilerParams(
            collective_id=0, has_side_effects=True, vmem_limit_bytes=56 * 2**20
        ),
    )(
        patches,
        jnp.concatenate([v.astype(F32) for v in (ln_gain, ln_bias, merge_bias)])[None, :],
        jnp.swapaxes(merge_weight, 1, 2),
        targets[None, :],
        text_embed,
    )


def solution(mesh):
    in_specs = (
        P("tp", "seq"),
        P("tp"),
        P("tp"),
        P(None, "tp", "seq"),
        P("tp"),
        P("seq"),
        P("tp", "seq"),
    )
    out_specs = P("tp", "seq")
    return jax.shard_map(shards, mesh=mesh, in_specs=in_specs, out_specs=out_specs, check_vma=False)
```

```python
import functools

import jax
import jax.numpy as jnp
from jax import lax
from jax.experimental import pallas as pl
from jax.experimental.pallas import tpu as pltpu
from jax.sharding import PartitionSpec as P

D = 1664
GROUP = 4
LANES = 128
MESH = pl.DeviceIdType.MESH
F32 = jnp.float32
BF16 = jnp.bfloat16


def contract(lhs, rhs, lhs_dim, rhs_dim):
    return lax.dot_general(
        lhs, rhs, (((lhs_dim,), (rhs_dim,)), ((), ())), preferred_element_type=F32
    )


def round_up(value, unit):
    return -(-value // unit) * unit


def split_columns(feats, shard_cols):
    main = feats // LANES * LANES
    rest = feats - main
    if main and rest and LANES % rest == 0 and shard_cols > 64:
        fold = LANES // rest
        sizes = [64, shard_cols - 64]
        if all(GROUP * size % (16 * fold) == 0 and size % 8 == 0 for size in sizes) and 64 % (16 * fold) == 0:
            return sizes, main, fold
    return [shard_cols], feats, 0


def payload_rows(slots, size):
    full, rest = divmod(size, LANES)
    total = full * slots
    if rest:
        fold = LANES // rest if LANES % rest == 0 else 1
        total += 8 * (-(-(slots // 8) // fold))
    return round_up(total, 16)


def pack_rows(rows, slots, size):
    full, rest = divmod(size, LANES)
    parts = [rows[:, q * LANES : (q + 1) * LANES] for q in range(full)]
    if rest:
        fold = LANES // rest if LANES % rest == 0 else 1
        groups = [rows[8 * g : 8 * g + 8, full * LANES :] for g in range(slots // 8)]
        for g in range(0, len(groups), fold):
            line = groups[g : g + fold]
            short = LANES - rest * len(line)
            if short:
                line = line + [jnp.zeros((8, short), F32)]
            parts.append(jnp.concatenate(line, axis=1))
    have = sum(part.shape[0] for part in parts)
    if have < payload_rows(slots, size):
        parts.append(jnp.zeros((payload_rows(slots, size) - have, LANES), F32))
    return jnp.concatenate(parts, axis=0)


def unpack_rows(stack, slots, size):
    full, rest = divmod(size, LANES)
    parts = [stack[q * slots : (q + 1) * slots] for q in range(full)]
    if rest:
        fold = LANES // rest if LANES % rest == 0 else 1
        base = full * slots
        groups = []
        for g in range(slots // 8):
            line = base + 8 * (g // fold)
            lane = (g % fold) * rest
            groups.append(stack[line : line + 8, lane : lane + rest])
        parts.append(jnp.concatenate(groups, axis=0))
    return jnp.concatenate(parts, axis=1)


def merge_kernel(
    nseq, ntp, slots, npieces, nchunks,
    x_ref, gain_ref, bias_ref, mbias_ref, w_ref, trow_ref, text_ref,
    out_ref,
    stats, xs, tok, w_low, wpl0, wpl1, psend, cores, summed, parts, mcol, pick, posend, posbuf, place,
    s_w, r_w, s_z, r_z, s_t, r_t, s_st, r_st, s_c, r_c, s_p, r_p, s_d, r_d, s_pos, r_pos,
    *buffers,
):
    me, tp = lax.axis_index("seq"), lax.axis_index("tp")
    plane, member = me // GROUP, lax.rem(me, GROUP)
    planes = nseq // GROUP
    owned = planes // ntp
    feats, tokens = x_ref.shape
    rows = tokens // GROUP
    prompt_rows = text_ref.shape[1]
    shard_cols = w_ref.shape[1]
    block_cols = shard_cols * GROUP
    sizes, main, fold = split_columns(feats, shard_cols)
    chunks = []
    for size in sizes:
        chunks.append((sum(n for _, n in chunks), GROUP * size))
    per = 2 if fold else 1
    wbuf = [buffers[c * per : (c + 1) * per] for c in range(nchunks)]
    send = buffers[npieces : npieces + nchunks]
    got = buffers[npieces + nchunks :]

    def remote(src, dst, send_sem, recv_sem, seq_id, tp_id):
        return pltpu.make_async_remote_copy(
            src_ref=src, dst_ref=dst, send_sem=send_sem, recv_sem=recv_sem,
            device_id=(seq_id, tp_id), device_id_type=MESH,
        )

    barrier = pltpu.get_barrier_semaphore()

    @pl.loop(0, nseq)
    def _(other):
        @pl.when(other != me)
        def _():
            pl.semaphore_signal(barrier, inc=1, device_id=(other, tp), device_id_type=MESH)

    for other_tp in range(ntp):
        @pl.when(other_tp != tp)
        def _():
            for i in range(GROUP):
                pl.semaphore_signal(
                    barrier, inc=1, device_id=(plane * GROUP + i, other_tp), device_id_type=MESH
                )
    pl.semaphore_wait(barrier, nseq - 1 + GROUP * (ntp - 1))

    first_cols = sizes[0]

    def weight_copy(i, c, slot):
        if c:
            src, dst = w_low.at[i], wpl1.at[slot]
        else:
            src = w_ref.at[i, pl.ds(0, first_cols)] if nchunks > 1 else w_ref.at[i]
            dst = wpl0.at[slot]
        return remote(src, dst, s_w.at[c, i], r_w.at[c, slot], plane * GROUP + i, tp)

    def send_weight(c):
        for i in range(GROUP):
            @pl.when(i != member)
            def _():
                weight_copy(i, c, member).start()

    def wait_weight(c):
        for i in range(GROUP):
            @pl.when(i != member)
            def _():
                weight_copy(i, c, i).wait_recv()

    def fold_lanes(rows_in):
        part = rows_in.shape[0] // fold
        return jnp.concatenate(
            [rows_in[q * part : (q + 1) * part, main:] for q in range(fold)], axis=1
        ).astype(BF16)

    def unfold_lanes(folded):
        lanes = LANES // fold
        return jnp.concatenate(
            [folded[:, q * lanes : (q + 1) * lanes] for q in range(fold)], axis=0
        )

    def put_first(slot, rows_in):
        wbuf[0][0][plane, slot] = rows_in[:, :main]
        if fold:
            wbuf[0][1][plane, slot] = fold_lanes(rows_in)

    moves = 2 + (nchunks - 1)

    def relay(zz, move, up):
        target = (plane + 1 if up else plane - 1) * GROUP + member
        way = 1 if up else 0
        copies = []
        for q, ref in enumerate(wbuf[move // 2]):
            view = (ref.at[zz, 0], ref.at[zz, pl.ds(1, GROUP - 1)], ref.at[zz])[move]
            copies.append(
                remote(
                    view, view, s_z.at[way, zz, move * per + q], r_z.at[zz, move * per + q],
                    target, tp,
                )
            )
        return copies

    def pass_on(zz, move, act):
        @pl.when((zz <= plane) & (plane + 1 < planes))
        def _():
            for copy in relay(zz, move, True):
                act(copy)

        @pl.when((zz >= plane) & (plane > 0))
        def _():
            for copy in relay(zz, move, False):
                act(copy)

    def take_and_pass(far, move):
        @pl.loop(0, 2)
        def _(side):
            zz = plane + (2 * side - 1) * far

            @pl.when((zz >= 0) & (zz < planes))
            def _():
                for copy in relay(zz, move, True):
                    copy.wait_recv()
                pass_on(zz, move, lambda copy: copy.start())

    send_weight(0)
    put_first(0, w_ref[member][:first_cols])
    pass_on(plane, 0, lambda copy: copy.start())
    if nchunks > 1:
        for i in range(GROUP):
            w_low[i, 0 : sizes[1]] = w_ref[i, first_cols:]
            if w_low.shape[1] > sizes[1]:
                w_low[i, sizes[1] :] = jnp.zeros((w_low.shape[1] - sizes[1], feats), BF16)
        send_weight(1)

    chunk = 256

    @pl.loop(0, tokens // chunk)
    def _(c):
        at = pl.ds(pl.multiple_of(c * chunk, chunk), chunk)
        values = x_ref[:, at].astype(F32)
        mean = jnp.sum(values, axis=0, keepdims=True) / feats
        apart = values - mean
        stats[tp, 0:1, at] = mean
        stats[tp, 1:2, at] = jnp.sum(apart * apart, axis=0, keepdims=True)

    def stats_copy(other_tp, slot):
        return remote(
            stats.at[slot], stats.at[slot], s_st.at[other_tp], r_st.at[slot], me, other_tp
        )

    for other_tp in range(ntp):
        @pl.when(other_tp != tp)
        def _():
            stats_copy(other_tp, tp).start()

    wait_weight(0)
    for r in range(1, GROUP):
        put_first(r, wpl0[lax.rem(member + r, GROUP)])
    pass_on(plane, 1, lambda copy: copy.start())
    for other_tp in range(ntp):
        @pl.when(other_tp != tp)
        def _():
            stats_copy(other_tp, other_tp).wait_recv()
    columns = jnp.concatenate(
        [ref[...].astype(F32).reshape(1, feats) for ref in (gain_ref, bias_ref, mbias_ref)]
        + [jnp.zeros((5, feats), F32)],
        axis=0,
    ).T
    gain, bias = columns[:, 0:1], columns[:, 1:2]
    for b in range(owned):
        for c, (row0, size) in enumerate(chunks):
            for i in range(GROUP):
                come = b * block_cols + i * shard_cols + sum(sizes[:c])
                go = b * block_cols + row0 + i * sizes[c]
                mcol[go : go + sizes[c]] = jnp.broadcast_to(
                    columns[come : come + sizes[c], 2:3], (sizes[c], LANES)
                )
    wide = GROUP * LANES
    from_tok = lax.broadcasted_iota(jnp.int32, (wide, wide), 0)
    to_tok = lax.broadcasted_iota(jnp.int32, (wide, wide), 1)
    sorter = (from_tok == GROUP * (to_tok % LANES) + to_tok // LANES).astype(F32).astype(BF16)
    for c in range(tokens // wide):
        at = slice(c * wide, (c + 1) * wide)
        mean = sum(stats[q, 0:1, at] for q in range(ntp)) / ntp
        square = sum(
            stats[q, 1:2, at] + feats * (stats[q, 0:1, at] - mean) ** 2 for q in range(ntp)
        )
        scale = lax.rsqrt(square / (feats * ntp) + 1e-06)
        normed = (
            (x_ref[:, at].astype(F32) - mean) * scale * gain + bias
        ).astype(BF16)
        by_patch = jnp.dot(normed, sorter, preferred_element_type=F32).astype(BF16)
        for i in range(GROUP):
            xs[i, :, c * LANES : (c + 1) * LANES] = by_patch[:, i * LANES : (i + 1) * LANES]

    def token_copy(i, slot, sem):
        return remote(xs.at[i], tok.at[slot], s_t.at[i], r_t.at[sem], plane * GROUP + i, tp)

    for i in range(GROUP):
        @pl.when(i != member)
        def _():
            token_copy(i, member, member).start()
    tok[member] = xs[member]

    if nchunks > 1:
        wait_weight(1)
        wpl1[member] = w_low[member]
        low = jnp.concatenate(
            [wpl1[i].astype(F32)[: sizes[1]] for i in range(GROUP)], axis=0
        )
        wbuf[1][0][plane] = low[:, :main].astype(BF16)
        wbuf[1][1][plane] = fold_lanes(low)
        pass_on(plane, 2, lambda copy: copy.start())

    def core_copy(zz, c):
        home = zz // owned
        at = pl.ds(*chunks[c])
        return remote(
            psend.at[zz, :, at], cores.at[zz - home * owned, tp, :, at],
            s_c.at[zz, c], r_c.at[zz - home * owned, c, tp], me, home,
        )

    def part_copy(b, c, i):
        at = pl.ds(*chunks[c])
        return remote(
            summed.at[b, i, at], parts.at[b, member, at],
            s_p.at[b, c, i], r_p.at[b, c, member], plane * GROUP + i, tp,
        )

    def use_chunk(zz, c):
        at = pl.ds(*chunks[c])
        if c:
            weight = jnp.concatenate([wbuf[1][0][zz], unfold_lanes(wbuf[1][1][zz])], axis=1)
        else:
            members = []
            for i in range(GROUP):
                slot = lax.rem(i - member + GROUP, GROUP)
                piece = wbuf[0][0][zz, slot]
                if fold:
                    piece = jnp.concatenate([piece, unfold_lanes(wbuf[0][1][zz, slot])], axis=1)
                members.append(piece if fold else piece.astype(F32))
            weight = jnp.concatenate(members, axis=0).astype(BF16)
        for i in range(GROUP):
            psend[zz, i, at] = contract(weight, tok[i], 1, 0).astype(BF16)

        @pl.when(zz // owned != tp)
        def _():
            core_copy(zz, c).start()

    def join_chunk(zz, c):
        b = zz - tp * owned
        at = pl.ds(*chunks[c])
        for q in range(ntp):
            @pl.when(q != tp)
            def _():
                remote(
                    psend.at[zz, :, at], cores.at[b, q, :, at], s_c.at[zz, c], r_c.at[b, c, q], me, q
                ).wait_recv()

            @pl.when(q == tp)
            def _():
                cores[b, q, :, at] = psend[zz, :, at]
        for i in range(GROUP):
            total = sum(cores[b, q, i, at].astype(F32) for q in range(ntp))
            summed[b, i, at] = total.astype(BF16)

            @pl.when(i != member)
            def _():
                part_copy(b, c, i).start()

            @pl.when(i == member)
            def _():
                parts[b, member, at] = summed[b, i, at]

    def row_copy(b, c, other, slot):
        return remote(
            send[c].at[b, other], got[c].at[b, slot],
            s_d.at[b, c, other], r_d.at[b, c, slot], other, tp,
        )

    def place_chunk(zz, c):
        b = zz - tp * owned
        row0, size = chunks[c]
        at = pl.ds(row0, size)
        total = jnp.zeros((size, rows), F32)
        for i in range(GROUP):
            @pl.when(i != member)
            def _():
                remote(
                    summed.at[b, i, at], parts.at[b, i, at],
                    s_p.at[b, c, i], r_p.at[b, c, i], plane * GROUP + i, tp,
                ).wait_recv()
            total = total + parts[b, i, at].astype(F32)
        shift = mcol[pl.ds(pl.multiple_of(b * block_cols + row0, 8), size), :][:, 0:1]
        merged = (total + shift).T.astype(BF16)

        @pl.loop(0, planes)
        def _(step):
            to = lax.rem(plane + planes // 2 + step, planes)
            picked = contract(pick[to], merged, 1, 0)
            for i in range(GROUP):
                other = to * GROUP + i
                send[c][b, other] = pack_rows(
                    picked[i * slots : (i + 1) * slots], slots, size
                ).astype(BF16)

                @pl.when(other != me)
                def _():
                    row_copy(b, c, other, me).start()

                @pl.when(other == me)
                def _():
                    got[c][b, me] = send[c][b, me]

    def both_sides(far, act):
        @pl.loop(0, 2)
        def _(side):
            zz = plane + (2 * side - 1) * far

            @pl.when((zz >= 0) & (zz < planes) & ((far > 0) | (side == 0)))
            def _():
                act(zz)

    def owned_sides(far, c, act):
        def act_owned(zz):
            @pl.when(zz // owned == tp)
            def _():
                act(zz, c)

        both_sides(far, act_owned)

    take_and_pass(1, 0)
    take_and_pass(1, 1)

    trow = trow_ref[...]
    tcol = jnp.broadcast_to(trow.astype(F32), (8, rows)).T[:, 0:1].astype(jnp.int32)
    dest_row = trow // prompt_rows
    dest_col = tcol // prompt_rows
    first = lax.broadcasted_iota(jnp.int32, (rows, rows), 0)
    second = lax.broadcasted_iota(jnp.int32, (rows, rows), 1)
    same = dest_col == dest_row
    order_row = jnp.sum((same & (first < second)).astype(F32), axis=0, keepdims=True)
    order_col = jnp.sum((same & (second < first)).astype(F32), axis=1, keepdims=True)
    slot_row = dest_row * slots + order_row.astype(jnp.int32)
    slot_col = dest_col * slots + order_col.astype(jnp.int32)
    local_col = (tcol - dest_col * prompt_rows + 1).astype(F32)

    @pl.loop(0, planes)
    def _(to):
        size = GROUP * slots
        slot_at = to * size + lax.broadcasted_iota(jnp.int32, (size, rows), 0)
        pick[to] = (slot_at == slot_row).astype(F32).astype(BF16)

    if moves > 2:
        take_and_pass(1, 2)

    def pos_copy(other, slot):
        return remote(
            posend.at[other], posbuf.at[slot], s_pos.at[other], r_pos.at[slot], other, tp
        )

    @pl.loop(0, nseq)
    def _(other):
        base = other * slots
        lane = lax.broadcasted_iota(jnp.int32, (rows, LANES), 1)
        held = jnp.where((slot_col == base + lane) & (lane < slots), local_col, 0.0)
        posend[other] = jnp.broadcast_to(jnp.sum(held, axis=0, keepdims=True), (8, LANES))

        @pl.when(other != me)
        def _():
            pos_copy(other, me).start()

        @pl.when(other == me)
        def _():
            posbuf[me] = posend[me]

    for i in range(GROUP):
        @pl.when(i != member)
        def _():
            token_copy(i, i, i).wait_recv()

    @pl.loop(0, planes)
    def _(far):
        for c in range(nchunks):
            @pl.when(far > 1)
            def _():
                for move in (2,) if c else (0, 1):
                    take_and_pass(far, move)
            both_sides(far, lambda zz: use_chunk(zz, c))
            owned_sides(far, c, join_chunk)
            if c:
                owned_sides(far, c - 1, place_chunk)
            else:
                @pl.when(far > 0)
                def _():
                    owned_sides(far - 1, nchunks - 1, place_chunk)

    diagonal = lax.broadcasted_iota(jnp.int32, (slots, LANES), 0) == lax.broadcasted_iota(
        jnp.int32, (slots, LANES), 1
    )
    position = (
        lax.broadcasted_iota(jnp.int32, (GROUP * slots, prompt_rows), 1).astype(F32) + 1.0
    )

    def spots(source, hits):
        lines = []
        for i in range(GROUP):
            other = source * GROUP + i

            @pl.when(other != me)
            def _():
                pos_copy(other, other).wait_recv()
            line = posbuf[other][0:1]
            lines.append(jnp.sum(jnp.where(diagonal, line, 0.0), axis=1, keepdims=True))
        spot = (jnp.concatenate(lines, axis=0) == position).astype(F32)
        place[source] = spot.astype(BF16)
        return hits + jnp.sum(spot, axis=0, keepdims=True)

    hits = lax.fori_loop(0, planes, spots, jnp.zeros((1, prompt_rows), F32))
    owned_sides(planes - 1, nchunks - 1, place_chunk)

    @pl.loop(0, owned)
    def _(turn):
        b = jnp.where(2 * tp < ntp, owned - 1 - turn, turn)
        images = []
        for c, (row0, size) in enumerate(chunks):
            @pl.loop(0, nseq)
            def _(other):
                @pl.when(other != me)
                def _():
                    row_copy(b, c, other, other).wait_recv()
            arrived = jnp.concatenate(
                [unpack_rows(got[c][b, s].astype(F32), slots, size) for s in range(nseq)], axis=0
            ).astype(BF16)
            images.append(
                contract(arrived, place[...].reshape(nseq * slots, prompt_rows), 0, 0)
            )
        image = jnp.concatenate(
            [
                images[c][i * sizes[c] : (i + 1) * sizes[c]]
                for i in range(GROUP)
                for c in range(nchunks)
            ],
            axis=0,
        )
        at = pl.ds(pl.multiple_of(b * block_cols, 8), block_cols)
        out_ref[at, :] = jnp.where(hits > 0.5, image.astype(BF16), text_ref[at, :])

    for i in range(GROUP):
        @pl.when(i != member)
        def _():
            for c in range(nchunks):
                weight_copy(i, c, member).wait_send()
            token_copy(i, member, member).wait_send()
    for other_tp in range(ntp):
        @pl.when(other_tp != tp)
        def _():
            stats_copy(other_tp, tp).wait_send()

    @pl.loop(0, planes)
    def _(zz):
        for move in range(moves):
            pass_on(zz, move, lambda copy: copy.wait_send())
        for c in range(nchunks):

            @pl.when(zz // owned != tp)
            def _():
                core_copy(zz, c).wait_send()

            @pl.when(zz // owned == tp)
            def _():
                for i in range(GROUP):
                    @pl.when(i != member)
                    def _():
                        part_copy(zz - tp * owned, c, i).wait_send()

    @pl.loop(0, nseq)
    def _(other):
        @pl.when(other != me)
        def _():
            pos_copy(other, me).wait_send()
            for b in range(owned):
                for c in range(nchunks):
                    row_copy(b, c, other, me).wait_send()


def shards(patches, ln_gain, ln_bias, merge_weight, merge_bias, targets, text_embed):
    nseq, ntp = lax.axis_size("seq"), lax.axis_size("tp")
    feats, tokens = patches.shape
    rows = tokens // GROUP
    shard_cols = merge_weight.shape[2]
    planes = nseq // GROUP
    owned = planes // ntp
    block_cols = GROUP * shard_cols
    prompt_rows = text_embed.shape[1]
    slots = round_up(5 * rows // (2 * nseq), 8)
    sizes, main, fold = split_columns(feats, shard_cols)
    chunks = [(0, GROUP * size) for size in sizes]
    low_rows = round_up(sizes[-1], 16)
    pieces = [pltpu.VMEM((planes, GROUP, sizes[0], main), BF16)]
    if fold:
        pieces += [
            pltpu.VMEM((planes, GROUP, sizes[0] // fold, LANES), BF16),
            pltpu.VMEM((planes, GROUP * sizes[1], main), BF16),
            pltpu.VMEM((planes, GROUP * sizes[1] // fold, LANES), BF16),
        ]
    payloads = [
        pltpu.VMEM((owned, nseq, payload_rows(slots, size), LANES), BF16)
        for _, size in chunks
    ]
    dma = pltpu.SemaphoreType.DMA
    count = len(chunks)
    return pl.pallas_call(
        functools.partial(merge_kernel, nseq, ntp, slots, len(pieces), count),
        out_shape=jax.ShapeDtypeStruct(text_embed.shape, text_embed.dtype),
        in_specs=[pl.BlockSpec(memory_space=pltpu.VMEM)] * 7,
        out_specs=pl.BlockSpec(memory_space=pltpu.VMEM),
        scratch_shapes=[
            pltpu.VMEM((ntp, 2, tokens), F32),
            pltpu.VMEM((GROUP, feats, rows), BF16),
            pltpu.VMEM((GROUP, feats, rows), BF16),
            pltpu.VMEM((GROUP, low_rows, feats), BF16),
            pltpu.VMEM((GROUP, sizes[0], feats), BF16),
            pltpu.VMEM((GROUP, low_rows, feats), BF16),
            pltpu.VMEM((planes, GROUP, block_cols, rows), BF16),
            pltpu.VMEM((owned, ntp, GROUP, block_cols, rows), BF16),
            pltpu.VMEM((owned, GROUP, block_cols, rows), BF16),
            pltpu.VMEM((owned, GROUP, block_cols, rows), BF16),
            pltpu.VMEM((feats, LANES), F32),
            pltpu.VMEM((planes, GROUP * slots, rows), BF16),
            pltpu.VMEM((nseq, 8, LANES), F32),
            pltpu.VMEM((nseq, 8, LANES), F32),
            pltpu.VMEM((planes, GROUP * slots, prompt_rows), BF16),
            dma((2, GROUP)), dma((2, GROUP)),
            dma((2, planes, 6)), dma((planes, 6)),
            dma((GROUP,)), dma((GROUP,)),
            dma((ntp,)), dma((ntp,)),
            dma((planes, count)), dma((owned, count, ntp)),
            dma((owned, count, GROUP)), dma((owned, count, GROUP)),
            dma((owned, count, nseq)), dma((owned, count, nseq)),
            dma((nseq,)), dma((nseq,)),
        ] + pieces + payloads + payloads,
        compiler_params=pltpu.CompilerParams(
            collective_id=0, has_side_effects=True, vmem_limit_bytes=56 * 2**20
        ),
    )(
        patches,
        ln_gain,
        ln_bias,
        merge_bias,
        jnp.swapaxes(merge_weight, 1, 2),
        targets[None, :],
        text_embed,
    )


def solution(mesh):
    in_specs = (
        P("tp", "seq"),
        P("tp"),
        P("tp"),
        P(None, "tp", "seq"),
        P("tp"),
        P("seq"),
        P("tp", "seq"),
    )
    out_specs = P("tp", "seq")
    return jax.shard_map(shards, mesh=mesh, in_specs=in_specs, out_specs=out_specs, check_vma=False)
```

```python
import functools

import jax
import jax.numpy as jnp
from jax import lax
from jax.experimental import pallas as pl
from jax.experimental.pallas import tpu as pltpu
from jax.sharding import PartitionSpec as P

D = 1664
GROUP = 4
LANES = 128
MESH = pl.DeviceIdType.MESH
F32 = jnp.float32
BF16 = jnp.bfloat16


def contract(lhs, rhs, lhs_dim, rhs_dim):
    return lax.dot_general(
        lhs, rhs, (((lhs_dim,), (rhs_dim,)), ((), ())), preferred_element_type=F32
    )


def round_up(value, unit):
    return -(-value // unit) * unit


def split_columns(feats, shard_cols):
    main = feats // LANES * LANES
    rest = feats - main
    if main and rest and LANES % rest == 0 and shard_cols > 64:
        fold = LANES // rest
        sizes = [64, shard_cols - 64]
        if all(GROUP * size % (16 * fold) == 0 and size % 8 == 0 for size in sizes) and 64 % (16 * fold) == 0:
            return sizes, main, fold
    return [shard_cols], feats, 0


def payload_rows(slots, size):
    full, rest = divmod(size, LANES)
    total = full * slots
    if rest:
        fold = LANES // rest if LANES % rest == 0 else 1
        total += 8 * (-(-(slots // 8) // fold))
    return round_up(total, 16)


def pack_rows(rows, slots, size):
    full, rest = divmod(size, LANES)
    parts = [rows[:, q * LANES : (q + 1) * LANES] for q in range(full)]
    if rest:
        fold = LANES // rest if LANES % rest == 0 else 1
        groups = [rows[8 * g : 8 * g + 8, full * LANES :] for g in range(slots // 8)]
        for g in range(0, len(groups), fold):
            line = groups[g : g + fold]
            short = LANES - rest * len(line)
            if short:
                line = line + [jnp.zeros((8, short), F32)]
            parts.append(jnp.concatenate(line, axis=1))
    have = sum(part.shape[0] for part in parts)
    if have < payload_rows(slots, size):
        parts.append(jnp.zeros((payload_rows(slots, size) - have, LANES), F32))
    return jnp.concatenate(parts, axis=0)


def unpack_rows(stack, slots, size):
    full, rest = divmod(size, LANES)
    parts = [stack[q * slots : (q + 1) * slots] for q in range(full)]
    if rest:
        fold = LANES // rest if LANES % rest == 0 else 1
        base = full * slots
        groups = []
        for g in range(slots // 8):
            line = base + 8 * (g // fold)
            lane = (g % fold) * rest
            groups.append(stack[line : line + 8, lane : lane + rest])
        parts.append(jnp.concatenate(groups, axis=0))
    return jnp.concatenate(parts, axis=1)


def merge_kernel(
    nseq, ntp, slots, npieces, nchunks,
    x_ref, gain_ref, bias_ref, mbias_ref, w_ref, trow_ref, text_ref,
    out_ref,
    stats, xs, tok, w_low, wpl0, wpl1, psend, cores, summed, parts, mcol, pick, posend, posbuf, place,
    s_w, r_w, s_z, r_z, s_t, r_t, s_st, r_st, s_c, r_c, s_p, r_p, s_d, r_d, s_pos, r_pos,
    *buffers,
):
    me, tp = lax.axis_index("seq"), lax.axis_index("tp")
    plane, member = me // GROUP, lax.rem(me, GROUP)
    planes = nseq // GROUP
    owned = planes // ntp
    feats, tokens = x_ref.shape
    rows = tokens // GROUP
    prompt_rows = text_ref.shape[1]
    shard_cols = w_ref.shape[1]
    block_cols = shard_cols * GROUP
    sizes, main, fold = split_columns(feats, shard_cols)
    chunks = []
    for size in sizes:
        chunks.append((sum(n for _, n in chunks), GROUP * size))
    per = 2 if fold else 1
    wbuf = [buffers[c * per : (c + 1) * per] for c in range(nchunks)]
    send = buffers[npieces : npieces + nchunks]
    got = buffers[npieces + nchunks :]

    def remote(src, dst, send_sem, recv_sem, seq_id, tp_id):
        return pltpu.make_async_remote_copy(
            src_ref=src, dst_ref=dst, send_sem=send_sem, recv_sem=recv_sem,
            device_id=(seq_id, tp_id), device_id_type=MESH,
        )

    barrier = pltpu.get_barrier_semaphore()

    @pl.loop(0, nseq)
    def _(other):
        @pl.when(other != me)
        def _():
            pl.semaphore_signal(barrier, inc=1, device_id=(other, tp), device_id_type=MESH)

    for other_tp in range(ntp):
        @pl.when(other_tp != tp)
        def _():
            for i in range(GROUP):
                pl.semaphore_signal(
                    barrier, inc=1, device_id=(plane * GROUP + i, other_tp), device_id_type=MESH
                )
    pl.semaphore_wait(barrier, nseq - 1 + GROUP * (ntp - 1))

    first_cols = sizes[0]

    def weight_copy(i, c, slot):
        if c:
            src, dst = w_low.at[i], wpl1.at[slot]
        else:
            src = w_ref.at[i, pl.ds(0, first_cols)] if nchunks > 1 else w_ref.at[i]
            dst = wpl0.at[slot]
        return remote(src, dst, s_w.at[c, i], r_w.at[c, slot], plane * GROUP + i, tp)

    def send_weight(c):
        for i in range(GROUP):
            @pl.when(i != member)
            def _():
                weight_copy(i, c, member).start()

    def wait_weight(c):
        for i in range(GROUP):
            @pl.when(i != member)
            def _():
                weight_copy(i, c, i).wait_recv()

    def fold_lanes(rows_in):
        part = rows_in.shape[0] // fold
        return jnp.concatenate(
            [rows_in[q * part : (q + 1) * part, main:] for q in range(fold)], axis=1
        ).astype(BF16)

    def unfold_lanes(folded):
        lanes = LANES // fold
        return jnp.concatenate(
            [folded[:, q * lanes : (q + 1) * lanes] for q in range(fold)], axis=0
        )

    def put_first(slot, rows_in):
        wbuf[0][0][plane, slot] = rows_in[:, :main]
        if fold:
            wbuf[0][1][plane, slot] = fold_lanes(rows_in)

    moves = 2 + (nchunks - 1)

    def relay(zz, move, up):
        target = (plane + 1 if up else plane - 1) * GROUP + member
        way = 1 if up else 0
        copies = []
        for q, ref in enumerate(wbuf[move // 2]):
            view = (ref.at[zz, 0], ref.at[zz, pl.ds(1, GROUP - 1)], ref.at[zz])[move]
            copies.append(
                remote(
                    view, view, s_z.at[way, zz, move * per + q], r_z.at[zz, move * per + q],
                    target, tp,
                )
            )
        return copies

    def pass_on(zz, move, act):
        @pl.when((zz <= plane) & (plane + 1 < planes))
        def _():
            for copy in relay(zz, move, True):
                act(copy)

        @pl.when((zz >= plane) & (plane > 0))
        def _():
            for copy in relay(zz, move, False):
                act(copy)

    def take_and_pass(far, move):
        @pl.loop(0, 2)
        def _(side):
            zz = plane + (2 * side - 1) * far

            @pl.when((zz >= 0) & (zz < planes))
            def _():
                for copy in relay(zz, move, True):
                    copy.wait_recv()
                pass_on(zz, move, lambda copy: copy.start())

    send_weight(0)
    put_first(0, w_ref[member][:first_cols])
    pass_on(plane, 0, lambda copy: copy.start())
    if nchunks > 1:
        for i in range(GROUP):
            w_low[i, 0 : sizes[1]] = w_ref[i, first_cols:]
            if w_low.shape[1] > sizes[1]:
                w_low[i, sizes[1] :] = jnp.zeros((w_low.shape[1] - sizes[1], feats), BF16)
        send_weight(1)

    chunk = 256

    @pl.loop(0, tokens // chunk)
    def _(c):
        at = pl.ds(pl.multiple_of(c * chunk, chunk), chunk)
        values = x_ref[:, at].astype(F32)
        mean = jnp.sum(values, axis=0, keepdims=True) / feats
        apart = values - mean
        stats[tp, 0:1, at] = mean
        stats[tp, 1:2, at] = jnp.sum(apart * apart, axis=0, keepdims=True)

    def stats_copy(other_tp, slot):
        return remote(
            stats.at[slot], stats.at[slot], s_st.at[other_tp], r_st.at[slot], me, other_tp
        )

    for other_tp in range(ntp):
        @pl.when(other_tp != tp)
        def _():
            stats_copy(other_tp, tp).start()

    wait_weight(0)
    for r in range(1, GROUP):
        put_first(r, wpl0[lax.rem(member + r, GROUP)])
    pass_on(plane, 1, lambda copy: copy.start())
    for other_tp in range(ntp):
        @pl.when(other_tp != tp)
        def _():
            stats_copy(other_tp, other_tp).wait_recv()
    columns = jnp.concatenate(
        [ref[...].astype(F32).reshape(1, feats) for ref in (gain_ref, bias_ref, mbias_ref)]
        + [jnp.zeros((5, feats), F32)],
        axis=0,
    ).T
    gain, bias = columns[:, 0:1], columns[:, 1:2]
    for b in range(owned):
        for c, (row0, size) in enumerate(chunks):
            for i in range(GROUP):
                come = b * block_cols + i * shard_cols + sum(sizes[:c])
                go = b * block_cols + row0 + i * sizes[c]
                mcol[go : go + sizes[c]] = jnp.broadcast_to(
                    columns[come : come + sizes[c], 2:3], (sizes[c], LANES)
                )
    wide = GROUP * LANES
    from_tok = lax.broadcasted_iota(jnp.int32, (wide, wide), 0)
    to_tok = lax.broadcasted_iota(jnp.int32, (wide, wide), 1)
    sorter = (from_tok == GROUP * (to_tok % LANES) + to_tok // LANES).astype(F32).astype(BF16)
    for c in range(tokens // wide):
        at = slice(c * wide, (c + 1) * wide)
        mean = sum(stats[q, 0:1, at] for q in range(ntp)) / ntp
        square = sum(
            stats[q, 1:2, at] + feats * (stats[q, 0:1, at] - mean) ** 2 for q in range(ntp)
        )
        scale = lax.rsqrt(square / (feats * ntp) + 1e-06)
        normed = (
            (x_ref[:, at].astype(F32) - mean) * scale * gain + bias
        ).astype(BF16)
        by_patch = jnp.dot(normed, sorter, preferred_element_type=F32).astype(BF16)
        for i in range(GROUP):
            xs[i, :, c * LANES : (c + 1) * LANES] = by_patch[:, i * LANES : (i + 1) * LANES]

    def token_copy(i, slot, sem):
        return remote(xs.at[i], tok.at[slot], s_t.at[i], r_t.at[sem], plane * GROUP + i, tp)

    for i in range(GROUP):
        @pl.when(i != member)
        def _():
            token_copy(i, member, member).start()
    tok[member] = xs[member]

    if nchunks > 1:
        wait_weight(1)
        wpl1[member] = w_low[member]
        low = jnp.concatenate(
            [wpl1[i].astype(F32)[: sizes[1]] for i in range(GROUP)], axis=0
        )
        wbuf[1][0][plane] = low[:, :main].astype(BF16)
        wbuf[1][1][plane] = fold_lanes(low)
        pass_on(plane, 2, lambda copy: copy.start())

    def core_copy(zz, c):
        home = zz // owned
        at = pl.ds(*chunks[c])
        return remote(
            psend.at[zz, :, at], cores.at[zz - home * owned, tp, :, at],
            s_c.at[zz, c], r_c.at[zz - home * owned, c, tp], me, home,
        )

    def part_copy(b, c, i):
        at = pl.ds(*chunks[c])
        return remote(
            summed.at[b, i, at], parts.at[b, member, at],
            s_p.at[b, c, i], r_p.at[b, c, member], plane * GROUP + i, tp,
        )

    def use_chunk(zz, c):
        at = pl.ds(*chunks[c])
        if c:
            weight = jnp.concatenate([wbuf[1][0][zz], unfold_lanes(wbuf[1][1][zz])], axis=1)
        else:
            members = []
            for i in range(GROUP):
                slot = lax.rem(i - member + GROUP, GROUP)
                piece = wbuf[0][0][zz, slot]
                if fold:
                    piece = jnp.concatenate([piece, unfold_lanes(wbuf[0][1][zz, slot])], axis=1)
                members.append(piece if fold else piece.astype(F32))
            weight = jnp.concatenate(members, axis=0).astype(BF16)
        for i in range(GROUP):
            psend[zz, i, at] = contract(weight, tok[i], 1, 0).astype(BF16)

        @pl.when(zz // owned != tp)
        def _():
            core_copy(zz, c).start()

    def join_chunk(zz, c):
        b = zz - tp * owned
        at = pl.ds(*chunks[c])
        for q in range(ntp):
            @pl.when(q != tp)
            def _():
                remote(
                    psend.at[zz, :, at], cores.at[b, q, :, at], s_c.at[zz, c], r_c.at[b, c, q], me, q
                ).wait_recv()

            @pl.when(q == tp)
            def _():
                cores[b, q, :, at] = psend[zz, :, at]
        for i in range(GROUP):
            total = sum(cores[b, q, i, at].astype(F32) for q in range(ntp))
            summed[b, i, at] = total.astype(BF16)

            @pl.when(i != member)
            def _():
                part_copy(b, c, i).start()

            @pl.when(i == member)
            def _():
                parts[b, member, at] = summed[b, i, at]

    def row_copy(b, c, other, slot):
        return remote(
            send[c].at[b, other], got[c].at[b, slot],
            s_d.at[b, c, other], r_d.at[b, c, slot], other, tp,
        )

    def place_chunk(zz, c):
        b = zz - tp * owned
        row0, size = chunks[c]
        at = pl.ds(row0, size)
        total = jnp.zeros((size, rows), F32)
        for i in range(GROUP):
            @pl.when(i != member)
            def _():
                remote(
                    summed.at[b, i, at], parts.at[b, i, at],
                    s_p.at[b, c, i], r_p.at[b, c, i], plane * GROUP + i, tp,
                ).wait_recv()
            total = total + parts[b, i, at].astype(F32)
        shift = mcol[pl.ds(pl.multiple_of(b * block_cols + row0, 8), size), :][:, 0:1]
        merged = (total + shift).T.astype(BF16)

        @pl.loop(0, planes)
        def _(step):
            to = lax.rem(plane + planes // 2 + step, planes)
            picked = contract(pick[to], merged, 1, 0)
            for i in range(GROUP):
                other = to * GROUP + i
                send[c][b, other] = pack_rows(
                    picked[i * slots : (i + 1) * slots], slots, size
                ).astype(BF16)

                @pl.when(other != me)
                def _():
                    row_copy(b, c, other, me).start()

                @pl.when(other == me)
                def _():
                    got[c][b, me] = send[c][b, me]

    def both_sides(far, act):
        @pl.loop(0, 2)
        def _(side):
            zz = plane + (2 * side - 1) * far

            @pl.when((zz >= 0) & (zz < planes) & ((far > 0) | (side == 0)))
            def _():
                act(zz)

    def owned_sides(far, c, act):
        def act_owned(zz):
            @pl.when(zz // owned == tp)
            def _():
                act(zz, c)

        both_sides(far, act_owned)

    take_and_pass(1, 0)
    take_and_pass(1, 1)

    trow = trow_ref[...]
    tcol = jnp.broadcast_to(trow.astype(F32), (8, rows)).T[:, 0:1].astype(jnp.int32)
    dest_row = trow // prompt_rows
    dest_col = tcol // prompt_rows
    first = lax.broadcasted_iota(jnp.int32, (rows, rows), 0)
    second = lax.broadcasted_iota(jnp.int32, (rows, rows), 1)
    same = dest_col == dest_row
    order_row = jnp.sum((same & (first < second)).astype(F32), axis=0, keepdims=True)
    order_col = jnp.sum((same & (second < first)).astype(F32), axis=1, keepdims=True)
    slot_row = dest_row * slots + order_row.astype(jnp.int32)
    slot_col = dest_col * slots + order_col.astype(jnp.int32)
    local_col = (tcol - dest_col * prompt_rows + 1).astype(F32)

    @pl.loop(0, planes)
    def _(to):
        size = GROUP * slots
        slot_at = to * size + lax.broadcasted_iota(jnp.int32, (size, rows), 0)
        pick[to] = (slot_at == slot_row).astype(F32).astype(BF16)

    if moves > 2:
        take_and_pass(1, 2)

    def pos_copy(other, slot):
        return remote(
            posend.at[other], posbuf.at[slot], s_pos.at[other], r_pos.at[slot], other, tp
        )

    @pl.loop(0, nseq)
    def _(other):
        base = other * slots
        lane = lax.broadcasted_iota(jnp.int32, (rows, LANES), 1)
        held = jnp.where((slot_col == base + lane) & (lane < slots), local_col, 0.0)
        posend[other] = jnp.broadcast_to(jnp.sum(held, axis=0, keepdims=True), (8, LANES))

        @pl.when(other != me)
        def _():
            pos_copy(other, me).start()

        @pl.when(other == me)
        def _():
            posbuf[me] = posend[me]

    for i in range(GROUP):
        @pl.when(i != member)
        def _():
            token_copy(i, i, i).wait_recv()

    between = (plane > 0) & (plane + 1 < planes)

    @pl.loop(0, planes)
    def _(far):
        for c in range(nchunks):
            @pl.when((far > 1) & jnp.logical_not(between))
            def _():
                for move in (2,) if c else (0, 1):
                    take_and_pass(far, move)
            both_sides(far, lambda zz: use_chunk(zz, c))
            owned_sides(far, c, join_chunk)

            @pl.when((far > 0) & (far + 1 < planes) & between)
            def _():
                for move in (2,) if c else (0, 1):
                    take_and_pass(far + 1, move)
            if c:
                owned_sides(far, c - 1, place_chunk)
            else:
                @pl.when(far > 0)
                def _():
                    owned_sides(far - 1, nchunks - 1, place_chunk)

    diagonal = lax.broadcasted_iota(jnp.int32, (slots, LANES), 0) == lax.broadcasted_iota(
        jnp.int32, (slots, LANES), 1
    )
    position = (
        lax.broadcasted_iota(jnp.int32, (GROUP * slots, prompt_rows), 1).astype(F32) + 1.0
    )

    def spots(source, hits):
        lines = []
        for i in range(GROUP):
            other = source * GROUP + i

            @pl.when(other != me)
            def _():
                pos_copy(other, other).wait_recv()
            line = posbuf[other][0:1]
            lines.append(jnp.sum(jnp.where(diagonal, line, 0.0), axis=1, keepdims=True))
        spot = (jnp.concatenate(lines, axis=0) == position).astype(F32)
        place[source] = spot.astype(BF16)
        return hits + jnp.sum(spot, axis=0, keepdims=True)

    hits = lax.fori_loop(0, planes, spots, jnp.zeros((1, prompt_rows), F32))
    owned_sides(planes - 1, nchunks - 1, place_chunk)

    @pl.loop(0, owned)
    def _(turn):
        b = jnp.where(2 * tp < ntp, owned - 1 - turn, turn)
        images = []
        for c, (row0, size) in enumerate(chunks):
            @pl.loop(0, nseq)
            def _(other):
                @pl.when(other != me)
                def _():
                    row_copy(b, c, other, other).wait_recv()
            arrived = jnp.concatenate(
                [unpack_rows(got[c][b, s].astype(F32), slots, size) for s in range(nseq)], axis=0
            ).astype(BF16)
            images.append(
                contract(arrived, place[...].reshape(nseq * slots, prompt_rows), 0, 0)
            )
        image = jnp.concatenate(
            [
                images[c][i * sizes[c] : (i + 1) * sizes[c]]
                for i in range(GROUP)
                for c in range(nchunks)
            ],
            axis=0,
        )
        at = pl.ds(pl.multiple_of(b * block_cols, 8), block_cols)
        out_ref[at, :] = jnp.where(hits > 0.5, image.astype(BF16), text_ref[at, :])

    for i in range(GROUP):
        @pl.when(i != member)
        def _():
            for c in range(nchunks):
                weight_copy(i, c, member).wait_send()
            token_copy(i, member, member).wait_send()
    for other_tp in range(ntp):
        @pl.when(other_tp != tp)
        def _():
            stats_copy(other_tp, tp).wait_send()

    @pl.loop(0, planes)
    def _(zz):
        for move in range(moves):
            pass_on(zz, move, lambda copy: copy.wait_send())
        for c in range(nchunks):

            @pl.when(zz // owned != tp)
            def _():
                core_copy(zz, c).wait_send()

            @pl.when(zz // owned == tp)
            def _():
                for i in range(GROUP):
                    @pl.when(i != member)
                    def _():
                        part_copy(zz - tp * owned, c, i).wait_send()

    @pl.loop(0, nseq)
    def _(other):
        @pl.when(other != me)
        def _():
            pos_copy(other, me).wait_send()
            for b in range(owned):
                for c in range(nchunks):
                    row_copy(b, c, other, me).wait_send()


def shards(patches, ln_gain, ln_bias, merge_weight, merge_bias, targets, text_embed):
    nseq, ntp = lax.axis_size("seq"), lax.axis_size("tp")
    feats, tokens = patches.shape
    rows = tokens // GROUP
    shard_cols = merge_weight.shape[2]
    planes = nseq // GROUP
    owned = planes // ntp
    block_cols = GROUP * shard_cols
    prompt_rows = text_embed.shape[1]
    slots = round_up(5 * rows // (2 * nseq), 8)
    sizes, main, fold = split_columns(feats, shard_cols)
    chunks = [(0, GROUP * size) for size in sizes]
    low_rows = round_up(sizes[-1], 16)
    pieces = [pltpu.VMEM((planes, GROUP, sizes[0], main), BF16)]
    if fold:
        pieces += [
            pltpu.VMEM((planes, GROUP, sizes[0] // fold, LANES), BF16),
            pltpu.VMEM((planes, GROUP * sizes[1], main), BF16),
            pltpu.VMEM((planes, GROUP * sizes[1] // fold, LANES), BF16),
        ]
    payloads = [
        pltpu.VMEM((owned, nseq, payload_rows(slots, size), LANES), BF16)
        for _, size in chunks
    ]
    dma = pltpu.SemaphoreType.DMA
    count = len(chunks)
    return pl.pallas_call(
        functools.partial(merge_kernel, nseq, ntp, slots, len(pieces), count),
        out_shape=jax.ShapeDtypeStruct(text_embed.shape, text_embed.dtype),
        in_specs=[pl.BlockSpec(memory_space=pltpu.VMEM)] * 7,
        out_specs=pl.BlockSpec(memory_space=pltpu.VMEM),
        scratch_shapes=[
            pltpu.VMEM((ntp, 2, tokens), F32),
            pltpu.VMEM((GROUP, feats, rows), BF16),
            pltpu.VMEM((GROUP, feats, rows), BF16),
            pltpu.VMEM((GROUP, low_rows, feats), BF16),
            pltpu.VMEM((GROUP, sizes[0], feats), BF16),
            pltpu.VMEM((GROUP, low_rows, feats), BF16),
            pltpu.VMEM((planes, GROUP, block_cols, rows), BF16),
            pltpu.VMEM((owned, ntp, GROUP, block_cols, rows), BF16),
            pltpu.VMEM((owned, GROUP, block_cols, rows), BF16),
            pltpu.VMEM((owned, GROUP, block_cols, rows), BF16),
            pltpu.VMEM((feats, LANES), F32),
            pltpu.VMEM((planes, GROUP * slots, rows), BF16),
            pltpu.VMEM((nseq, 8, LANES), F32),
            pltpu.VMEM((nseq, 8, LANES), F32),
            pltpu.VMEM((planes, GROUP * slots, prompt_rows), BF16),
            dma((2, GROUP)), dma((2, GROUP)),
            dma((2, planes, 6)), dma((planes, 6)),
            dma((GROUP,)), dma((GROUP,)),
            dma((ntp,)), dma((ntp,)),
            dma((planes, count)), dma((owned, count, ntp)),
            dma((owned, count, GROUP)), dma((owned, count, GROUP)),
            dma((owned, count, nseq)), dma((owned, count, nseq)),
            dma((nseq,)), dma((nseq,)),
        ] + pieces + payloads + payloads,
        compiler_params=pltpu.CompilerParams(
            collective_id=0, has_side_effects=True, vmem_limit_bytes=56 * 2**20
        ),
    )(
        patches,
        ln_gain,
        ln_bias,
        merge_bias,
        jnp.swapaxes(merge_weight, 1, 2),
        targets[None, :],
        text_embed,
    )


def solution(mesh):
    in_specs = (
        P("tp", "seq"),
        P("tp"),
        P("tp"),
        P(None, "tp", "seq"),
        P("tp"),
        P("seq"),
        P("tp", "seq"),
    )
    out_specs = P("tp", "seq")
    return jax.shard_map(shards, mesh=mesh, in_specs=in_specs, out_specs=out_specs, check_vma=False)
```
